256 devices in a mesh: row: 16 (over x_lo, y, core), col: 16 (over z, x_hi).
Axes of the slice: x: 4 (x_hi: 2, x_lo: 2; x = x_hi * 2 + x_lo), y: 4, z: 8, core: 2. Of those that a mesh axis runs over, the one named last changes fastest.
Arguments:
- features: bfloat16 [65536, 128], P(('col', 'row')), may hold values from -6 to 6
- weight: bfloat16 [128, 256], replicated, may hold values from -0.5 to 0.5
- adj_tiles: bfloat16 [16, 16, 384, 128, 128], P('row', 'col'), may hold values from -0.125 to 0.125
- tile_row: int32 [16, 16, 384], P('row', 'col'), may hold values from 0 to 31
- tile_col: int32 [16, 16, 384], P('row', 'col'), may hold values from 0 to 31
- tile_count: int32 [16, 16], P('row', 'col'), may hold values from 48 to 384, as said below
- cotangent: bfloat16 [65536, 256], P(('row', 'col')), may hold values from -6 to 6
Outputs:
- activations: bfloat16 [65536, 256], P(('row', 'col'))
- feature_grad: bfloat16 [65536, 128], P(('col', 'row'))
- weight_grad: float32 [128, 256], replicated
The draws below stay inside these ranges and needn't reach their ends.
Inputs may be any that keep to these rules, and one draw needn't show every extreme that they name: `tile_count`: tiles in use on a device; some device uses all 384 slots.
All inputs are finite; a program needn't handle non-finite values.
Results may differ from the reference program's by a relative error of at most 0.023.
Values may be sent and summed in bfloat16 or wider, within the bound.
A program may use at most 128 MiB of HBM per device.

```python
import math
import jax
import jax.numpy as jnp
from jax import lax

F = 128
H = 256
TB = 128
BLK = 32
TMAX = 384
BLKC = 32
NODES = 65536
N_ROW = 16
N_COL = 16


def draw_tile_count(key, part):
    key = jax.random.fold_in(key, 5)
    first_key, second_key = jax.random.split(key)
    shifts = jax.random.randint(first_key, (N_ROW * N_COL,), 0, 4)
    counts = jnp.right_shift(jnp.full((N_ROW * N_COL,), TMAX, jnp.int32), shifts.astype(jnp.int32))
    chosen = jax.random.randint(second_key, (), 0, N_ROW * N_COL)
    counts = counts.at[chosen].set(TMAX)
    return counts.reshape(N_ROW, N_COL).astype(jnp.int32)


def set_ends(values, key, smallest, high):
    place = [jax.random.randint(jax.random.fold_in(key, axis), (), 0, length) for axis, length in enumerate(values.shape)]
    longest = values.shape.index(max(values.shape))
    next_to = place[:longest] + [(place[longest] + 1) % values.shape[longest]] + place[longest + 1:]
    return values.at[tuple(place)].set(smallest).at[tuple(next_to)].set(high)


def shard_levels(key, extent, pieces, least, high):
    def one(dim, shards_of):
        draws = jax.random.uniform(jax.random.fold_in(jax.random.fold_in(key, 6), dim), (shards_of,), jnp.float32, least / len(pieces), high / len(pieces))
        return jnp.repeat(jnp.exp(draws), extent[dim] // shards_of).reshape((-1,) + (1,) * (len(extent) - dim - 1))

    factor_of = one(*pieces[0])
    for cut in pieces[1:]:
        factor_of = factor_of * one(*cut)
    return factor_of


def noise(stream_key, dims, spread, limit, shards=(), kind=jnp.bfloat16):
    array = spread * jax.random.normal(stream_key, dims, jnp.float32)
    if shards:
        array = array * shard_levels(stream_key, dims, shards, -0.22, 0.18)
    return jnp.clip(array, -limit, limit).astype(kind)


def setup_inputs(seed: int = 0) -> dict:
    key_of = jax.random.split(jax.random.key(seed), 8)
    features = noise(key_of[0], (NODES, F), 1.0, 6.0, ((0, 256),))
    weight = noise(key_of[1], (F, H), F ** -0.5, 0.5)
    adj_tiles = noise(key_of[2], (N_ROW, N_COL, TMAX, TB, TB), ((TMAX * N_COL * TB // (2 * BLK)) ** -0.5), 0.125, ((0, 16), (1, 16)))
    tile_row = set_ends(jax.random.randint(key_of[3], (N_ROW, N_COL, TMAX), 0, BLK), jax.random.fold_in(key_of[3], 1), 0, BLK - 1).astype(jnp.int32)
    tile_col = set_ends(jax.random.randint(key_of[4], (N_ROW, N_COL, TMAX), 0, BLKC), jax.random.fold_in(key_of[4], 1), 0, BLKC - 1).astype(jnp.int32)
    tile_count = draw_tile_count(jax.random.fold_in(key_of[7], 71), 0)
    cotangent = noise(key_of[6], (NODES, H), 1.0, 6.0, ((0, 256),))
    return {"features": features, "weight": weight, "adj_tiles": adj_tiles, "tile_row": tile_row, "tile_col": tile_col, "tile_count": tile_count, "cotangent": cotangent}


def tile_sum(adj_block, lead_idx, trail_idx, tile_total, source, out_blocks, forward):
    picked_idx = trail_idx if forward else lead_idx
    placed_idx = lead_idx if forward else trail_idx
    pattern = 'tij,tjf->tif' if forward else 'tji,tjf->tif'
    gathered = jnp.take(source, picked_idx, axis=0).astype(jnp.float32)
    products = jnp.einsum(pattern, adj_block.astype(jnp.float32), gathered, precision=lax.Precision.HIGHEST)
    alive_mask = jnp.arange(TMAX, dtype=jnp.int32) < tile_total
    targets = jnp.arange(out_blocks, dtype=jnp.int32)
    one_hot = ((placed_idx[None, :] == targets[:, None]) & alive_mask[None, :]).astype(jnp.float32)
    return jnp.einsum('bt,tif->bif', one_hot, products, precision=lax.Precision.HIGHEST)

def reference(features, weight, adj_tiles, tile_row, tile_col, tile_count, cotangent):
    col_blocks = features.reshape(N_COL, BLKC, TB, F)

    def row_group(row_idx):

        def add_group(summed, col_idx):
            term = tile_sum(adj_tiles[row_idx, col_idx], tile_row[row_idx, col_idx], tile_col[row_idx, col_idx], tile_count[row_idx, col_idx], col_blocks[col_idx], BLK, True)
            return (summed + term, None)
        summed, unused = lax.scan(add_group, jnp.zeros((BLK, TB, F), jnp.float32), jnp.arange(N_COL, dtype=jnp.int32))
        return summed
    aggregated = lax.map(row_group, jnp.arange(N_ROW, dtype=jnp.int32)).reshape(NODES, F).astype(jnp.bfloat16)
    preact = jnp.dot(aggregated, weight, preferred_element_type=jnp.float32)
    sigma = jax.nn.sigmoid(preact)
    activations = (preact * sigma).astype(jnp.bfloat16)
    slope = sigma * (1.0 + preact * (1.0 - sigma))
    pre_grad = (cotangent.astype(jnp.float32) * slope).astype(jnp.bfloat16)
    weight_grad = lax.dot_general(aggregated, pre_grad, (((0,), (0,)), ((), ())), preferred_element_type=jnp.float32) / math.sqrt(NODES)
    agg_grad = jnp.dot(pre_grad, weight.T, preferred_element_type=jnp.float32).astype(jnp.bfloat16)
    row_blocks = agg_grad.reshape(N_ROW, BLK, TB, F)

    def col_group(col_idx):

        def add_group(summed, row_idx):
            term = tile_sum(adj_tiles[row_idx, col_idx], tile_row[row_idx, col_idx], tile_col[row_idx, col_idx], tile_count[row_idx, col_idx], row_blocks[row_idx], BLKC, False)
            return (summed + term, None)
        summed, unused = lax.scan(add_group, jnp.zeros((BLKC, TB, F), jnp.float32), jnp.arange(N_ROW, dtype=jnp.int32))
        return summed
    feature_grad = lax.map(col_group, jnp.arange(N_COL, dtype=jnp.int32)).reshape(NODES, F).astype(jnp.bfloat16)
    return (activations, feature_grad, weight_grad)
```

```python
import math

import jax
import jax.numpy as jnp
from jax import lax
from jax.experimental import pallas as pl
from jax.experimental.pallas import tpu as pltpu
from jax.sharding import PartitionSpec as P

F32 = jnp.float32
BF16 = jnp.bfloat16
MESH = pl.DeviceIdType.MESH

SIDE = 128
BLOCKS = 32
SLOTS = 384
PAIRS = (SLOTS + BLOCKS) // 2
ENTRIES = 512
GROUP = 16
UNROLL = 16
LOADS = 8
ZERO = BLOCKS
TILE, SOURCE, KEEP, LAST, SOME = range(5)


def upright(flat, lanes):
    column = jnp.transpose(jnp.broadcast_to(flat, (SIDE, flat.shape[1])))
    return jnp.concatenate([column] * (lanes // SIDE), axis=1)


def over_rows(condition, value):
    return jnp.sum(jnp.where(condition, value, 0), axis=0, keepdims=True)


def plan_pairs(place, pick, total):
    def counts(shape):
        return [lax.broadcasted_iota(jnp.int32, shape, d) for d in range(2)]

    place_up = upright(place, SLOTS)
    down, across = counts((SLOTS, SLOTS))
    rank = over_rows((place_up == place) & (down < total) & (down < across), 1)
    down, across = counts((SLOTS, SIDE))
    tiles = over_rows((place_up[:, :SIDE] == across) & (down < total), 1)
    pairs = (tiles + 1) // 2
    pairs_up = upright(pairs, SIDE)
    down, across = counts((SIDE, SIDE))
    first = over_rows(down < across, pairs_up)
    first_up = upright(first, ENTRIES)
    down, across = counts((BLOCKS, SLOTS))
    spot = rank + 2 * over_rows(down == place, first_up[:BLOCKS, :SLOTS])
    spot = jnp.where(lax.broadcasted_iota(jnp.int32, (1, SLOTS), 1) < total, spot, -1)
    down, across = counts((SLOTS, ENTRIES))
    found = upright(spot, ENTRIES) == across
    tile = over_rows(found, down)
    source = over_rows(found, upright(pick, ENTRIES) - ZERO) + ZERO
    down, across = counts((BLOCKS, ENTRIES))
    pairs_up = jnp.concatenate([pairs_up[:BLOCKS]] * (ENTRIES // SIDE), axis=1)
    keep = 1 - over_rows((first_up[:BLOCKS] == across) & (pairs_up > 0), 1)
    return tile, source, keep, jnp.maximum(first + pairs - 1, 0), jnp.minimum(pairs, 1)


def kernel(
    feat_hbm, weight_hbm, adj_hbm, row_hbm, col_hbm, count_hbm, cot_hbm,
    act_hbm, fgrad_hbm, wgrad_hbm,
    tiles, sums, xs, gs, weight, cot, rows, cols, plan_v, act_v, fgrad_v,
    col_out, col_in, col_sum, col_land, row_out, row_in, row_sum, row_land,
    wt, wt_land, wpart, wpart_land, wgrad_v,
    plan_f, plan_b, count,
    load_sem, small_sem, plan_sem, out_sem,
    ag1_send, ag1_recv, ag1f_send, ag1f_recv,
    rsx_send, rsx_recv, rsz_send, rsz_recv,
    ag2_send, ag2_recv, ag2f_send, ag2f_recv,
    rsc_send, rsc_recv, rsr_send, rsr_recv,
    w1_send, w1_recv, w2_send, w2_recv, w3_send, w3_recv,
):
    r = lax.axis_index("row")
    c = lax.axis_index("col")
    core, chip = r % 2, r // 2
    xlo, y = chip // 4, chip % 4
    xhi, z = c % 2, c // 2
    sibling = (2 * chip + (1 - core), c)
    partner = (r, 2 * z + (1 - xhi))

    def chip_at(k, sign):
        return 4 * ((xlo + k // 4) % 2) + (y + sign * (k % 4) + 4) % 4

    def z_at(k, sign):
        return (z + sign * k + 8) % 8

    def remote(src, dst, send, recv, device):
        return pltpu.make_async_remote_copy(
            src_ref=src, dst_ref=dst, send_sem=send, recv_sem=recv,
            device_id=device, device_id_type=MESH,
        )

    barrier = pltpu.get_barrier_semaphore()
    for k in range(1, GROUP):
        pl.semaphore_signal(barrier, inc=1, device_id=((r + k) % GROUP, c), device_id_type=MESH)
        pl.semaphore_signal(barrier, inc=1, device_id=(r, (c + k) % GROUP), device_id_type=MESH)

    smalls = [
        pltpu.make_async_copy(row_hbm.at[0, 0], rows.at[0], small_sem.at[0]),
        pltpu.make_async_copy(col_hbm.at[0, 0], cols.at[0], small_sem.at[1]),
        pltpu.make_async_copy(count_hbm, count, small_sem.at[2]),
        pltpu.make_async_copy(feat_hbm, xs.at[pl.ds(2 * r, 2)], small_sem.at[3]),
        pltpu.make_async_copy(weight_hbm, weight, small_sem.at[4]),
        pltpu.make_async_copy(cot_hbm, cot, small_sem.at[5]),
    ]
    for copy in smalls:
        copy.start()
    part = SLOTS // LOADS
    loads = [
        pltpu.make_async_copy(
            adj_hbm.at[0, 0, pl.ds(i * part, part)], tiles.at[pl.ds(i * part, part)], load_sem.at[i]
        )
        for i in range(LOADS)
    ]
    for copy in loads:
        copy.start()
    xs[ZERO] = jnp.zeros((SIDE, SIDE), BF16)
    gs[ZERO] = jnp.zeros((SIDE, SIDE), BF16)
    pl.semaphore_wait(barrier, 2 * (GROUP - 1))

    pending = []
    here = pl.ds(2 * r, 2)
    for k in range(8):
        device = sibling if k == 0 else (2 * chip_at(k, 1) + core, c)
        copy = remote(feat_hbm, xs.at[here], ag1_send.at[k], ag1_recv.at[k], device)
        copy.start()
        pending.append(copy)

    for copy in smalls[:3]:
        copy.wait()
    total = count[0, 0]
    plan_v[...] = jnp.zeros_like(plan_v)
    for i, (place, pick, ready) in enumerate(((rows, cols, plan_f), (cols, rows, plan_b))):
        listed = plan_pairs(place[...], pick[...], total)
        for j, value in enumerate(listed):
            plan_v[i, j : j + 1, : value.shape[1]] = value
        pltpu.make_async_copy(plan_v.at[i], ready, plan_sem.at[i]).start()

    forwards = []
    for k in range(1, 8):
        slot = xs.at[pl.ds(2 * (2 * chip_at(k, -1) + core), 2)]
        remote(slot, slot, ag1_send.at[k], ag1_recv.at[k], sibling).wait_recv()
        copy = remote(slot, slot, ag1f_send.at[k - 1], ag1f_recv.at[k - 1], sibling)
        copy.start()
        forwards.append(copy)
    slot = xs.at[pl.ds(2 * (2 * chip + 1 - core), 2)]
    remote(slot, slot, ag1_send.at[0], ag1_recv.at[0], sibling).wait_recv()
    for k in range(1, 8):
        slot = xs.at[pl.ds(2 * (2 * chip_at(k, -1) + 1 - core), 2)]
        remote(slot, slot, ag1f_send.at[k - 1], ag1f_recv.at[k - 1], sibling).wait_recv()
    for copy in smalls[3:]:
        copy.wait()
    for i in range(2):
        pltpu.make_async_copy(plan_v.at[i], (plan_f, plan_b)[i], plan_sem.at[i]).wait()
    for copy in loads:
        copy.wait()
    for copy in pending + forwards:
        copy.wait_send()

    def tile_pass(listed, source, forward):
        def some_pairs(turn, total):
            for u in range(UNROLL):
                p = turn * UNROLL + u
                one, two = tiles[listed[TILE, 2 * p]], tiles[listed[TILE, 2 * p + 1]]
                with_one, with_two = source[listed[SOURCE, 2 * p]], source[listed[SOURCE, 2 * p + 1]]
                if forward:
                    left = jnp.concatenate([one, two], axis=1)
                    right = jnp.concatenate([with_one, with_two], axis=0)
                else:
                    left = jnp.concatenate([with_one, with_two], axis=1)
                    right = jnp.concatenate([one, two], axis=0)
                product = jnp.dot(left, right, preferred_element_type=F32)
                total = total * listed[KEEP, p].astype(F32) + product
                sums[p] = total
            return total

        lax.fori_loop(0, PAIRS // UNROLL, some_pairs, jnp.zeros((SIDE, SIDE), F32))

    def block_sum(listed, b):
        return sums[listed[LAST, b]] * listed[SOME, b].astype(F32)

    tile_pass(plan_f, xs, True)
    order = (4, 3, 5, 2, 6, 1, 7, 0)
    pending = []
    for k in order:
        for h in range(2):
            b = 2 * (2 * z_at(k, 1) + 1 - xhi) + h
            col_out[k, h] = block_sum(plan_f, b).astype(BF16)
        copy = remote(col_out.at[k], col_in.at[k], rsx_send.at[k], rsx_recv.at[k], partner)
        copy.start()
        pending.append(copy)
    own = []
    for k in order:
        mine = [block_sum(plan_f, 2 * (2 * z_at(k, 1) + xhi) + h) for h in range(2)]
        remote(col_in.at[k], col_in.at[k], rsx_send.at[k], rsx_recv.at[k], partner).wait_recv()
        mine = [mine[h] + col_in[k, h].astype(F32) for h in range(2)]
        if k == 0:
            own = mine
        else:
            for h in range(2):
                col_sum[k, h] = mine[h].astype(BF16)
            copy = remote(
                col_sum.at[k], col_land.at[k], rsz_send.at[k - 1], rsz_recv.at[k - 1],
                (r, 2 * z_at(k, 1) + xhi),
            )
            copy.start()
            pending.append(copy)
    for k in (1, 7, 2, 6, 3, 5, 4):
        remote(
            col_land.at[k], col_land.at[k], rsz_send.at[k - 1], rsz_recv.at[k - 1], partner
        ).wait_recv()
        own = [own[h] + col_land[k, h].astype(F32) for h in range(2)]

    aggregated = jnp.concatenate(own, axis=0).astype(BF16)
    w = weight[...]
    preact = jnp.dot(aggregated, w, preferred_element_type=F32)
    sigma = jax.nn.sigmoid(preact)
    slope = sigma * (1.0 + preact * (1.0 - sigma))
    pre_grad = (cot[...].astype(F32) * slope).astype(BF16)
    agg_grad = lax.dot_general(
        w, pre_grad, (((1,), (1,)), ((), ())), preferred_element_type=F32
    ).astype(BF16)
    for h in range(2):
        gs[2 * c + h] = agg_grad[:, h * SIDE : (h + 1) * SIDE]

    here = pl.ds(2 * c, 2)
    ahead = (1, 7, 2, 6, 3, 5, 4)
    for k in ahead:
        copy = remote(
            gs.at[here], gs.at[here], ag2_send.at[k], ag2_recv.at[k], (r, 2 * z_at(k, 1) + xhi)
        )
        copy.start()
        pending.append(copy)
    copy = remote(gs.at[here], gs.at[here], ag2_send.at[0], ag2_recv.at[0], partner)
    copy.start()
    pending.append(copy)

    act_v[...] = (preact * sigma).astype(BF16)
    act_out = pltpu.make_async_copy(act_v, act_hbm, out_sem.at[0])
    act_out.start()
    terms = lax.dot_general(
        aggregated, pre_grad, (((0,), (0,)), ((), ())), preferred_element_type=F32
    )
    for q in range(GROUP):
        wt[q] = terms[8 * q : 8 * q + 8]
    for k in range(1, GROUP):
        to = (c + k) % GROUP
        copy = remote(wt.at[to], wt_land.at[k], w1_send.at[k], w1_recv.at[k], (r, to))
        copy.start()
        pending.append(copy)

    for k in ahead:
        slot = gs.at[pl.ds(2 * (2 * z_at(k, -1) + xhi), 2)]
        remote(slot, slot, ag2_send.at[k], ag2_recv.at[k], partner).wait_recv()
        copy = remote(slot, slot, ag2f_send.at[k - 1], ag2f_recv.at[k - 1], partner)
        copy.start()
        pending.append(copy)
    term = wt[c]
    for k in range(1, GROUP):
        remote(wt_land.at[k], wt_land.at[k], w1_send.at[k], w1_recv.at[k], partner).wait_recv()
        term = term + wt_land[k]
    wpart[...] = term
    for k in range(1, GROUP):
        copy = remote(
            wpart, wpart_land.at[k], w2_send.at[k], w2_recv.at[k], ((r + k) % GROUP, c)
        )
        copy.start()
        pending.append(copy)
    slot = gs.at[pl.ds(2 * (2 * z + 1 - xhi), 2)]
    remote(slot, slot, ag2_send.at[0], ag2_recv.at[0], partner).wait_recv()
    for k in ahead:
        slot = gs.at[pl.ds(2 * (2 * z_at(k, -1) + 1 - xhi), 2)]
        remote(slot, slot, ag2f_send.at[k - 1], ag2f_recv.at[k - 1], partner).wait_recv()

    tile_pass(plan_b, gs, False)
    order = (2, 6, 1, 3, 5, 7, 4, 0)
    for k in order:
        for h in range(2):
            b = 2 * (2 * chip_at(k, 1) + 1 - core) + h
            row_out[k, h] = block_sum(plan_b, b).astype(BF16)
        copy = remote(row_out.at[k], row_in.at[k], rsc_send.at[k], rsc_recv.at[k], sibling)
        copy.start()
        pending.append(copy)
    for k in order:
        mine = [block_sum(plan_b, 2 * (2 * chip_at(k, 1) + core) + h) for h in range(2)]
        remote(row_in.at[k], row_in.at[k], rsc_send.at[k], rsc_recv.at[k], sibling).wait_recv()
        mine = [mine[h] + row_in[k, h].astype(F32) for h in range(2)]
        if k == 0:
            own = mine
        else:
            for h in range(2):
                row_sum[k, h] = mine[h].astype(BF16)
            copy = remote(
                row_sum.at[k], row_land.at[k], rsr_send.at[k - 1], rsr_recv.at[k - 1],
                (2 * chip_at(k, 1) + core, c),
            )
            copy.start()
            pending.append(copy)

    term = wpart[...]
    for k in range(1, GROUP):
        remote(wpart_land.at[k], wpart_land.at[k], w2_send.at[k], w2_recv.at[k], partner).wait_recv()
        term = term + wpart_land[k]
    wgrad_v[c] = term * (1.0 / math.sqrt(SIDE * BLOCKS * GROUP))
    for k in range(1, GROUP):
        copy = remote(
            wgrad_v.at[c], wgrad_v.at[c], w3_send.at[k], w3_recv.at[k], (r, (c + k) % GROUP)
        )
        copy.start()
        pending.append(copy)

    for k in (1, 3, 4, 2, 5, 7, 6):
        remote(
            row_land.at[k], row_land.at[k], rsr_send.at[k - 1], rsr_recv.at[k - 1], sibling
        ).wait_recv()
        own = [own[h] + row_land[k, h].astype(F32) for h in range(2)]
    for h in range(2):
        fgrad_v[h * SIDE : (h + 1) * SIDE, :] = own[h].T.astype(BF16)
    fgrad_out = pltpu.make_async_copy(fgrad_v, fgrad_hbm, out_sem.at[1])
    fgrad_out.start()
    for k in range(1, GROUP):
        slot = wgrad_v.at[(c - k + GROUP) % GROUP]
        remote(slot, slot, w3_send.at[k], w3_recv.at[k], partner).wait_recv()
    wgrad_out = pltpu.make_async_copy(wgrad_v, wgrad_hbm, out_sem.at[2])
    wgrad_out.start()
    for copy in pending:
        copy.wait_send()
    act_out.wait()
    fgrad_out.wait()
    wgrad_out.wait()


def body(features, weight, adj_tiles, tile_row, tile_col, tile_count, cotangent):
    nodes, width = features.shape
    hidden = weight.shape[1]
    any_spec = pl.BlockSpec(memory_space=pl.ANY)
    dma = pltpu.SemaphoreType.DMA
    blocks = lambda *lead: pltpu.VMEM((*lead, SIDE, SIDE), BF16)
    act, fgrad, wgrad = pl.pallas_call(
        kernel,
        out_shape=(
            jax.ShapeDtypeStruct((nodes, hidden), BF16),
            jax.ShapeDtypeStruct((nodes, width), BF16),
            jax.ShapeDtypeStruct((GROUP, 8, hidden), F32),
        ),
        in_specs=[any_spec] * 7,
        out_specs=(any_spec,) * 3,
        scratch_shapes=[
            blocks(SLOTS),
            pltpu.VMEM((PAIRS, SIDE, SIDE), F32),
            blocks(BLOCKS + 1),
            blocks(BLOCKS + 1),
            pltpu.VMEM((width, hidden), BF16),
            pltpu.VMEM((nodes, hidden), BF16),
            pltpu.VMEM((1, SLOTS), jnp.int32),
            pltpu.VMEM((1, SLOTS), jnp.int32),
            pltpu.VMEM((2, 8, ENTRIES), jnp.int32),
            pltpu.VMEM((nodes, hidden), BF16),
            pltpu.VMEM((nodes, width), BF16),
            blocks(8, 2), blocks(8, 2), blocks(8, 2), blocks(8, 2),
            blocks(8, 2), blocks(8, 2), blocks(8, 2), blocks(8, 2),
            pltpu.VMEM((GROUP, 8, hidden), F32),
            pltpu.VMEM((GROUP, 8, hidden), F32),
            pltpu.VMEM((8, hidden), F32),
            pltpu.VMEM((GROUP, 8, hidden), F32),
            pltpu.VMEM((GROUP, 8, hidden), F32),
            pltpu.SMEM((8, ENTRIES), jnp.int32),
            pltpu.SMEM((8, ENTRIES), jnp.int32),
            pltpu.SMEM((1, 1), jnp.int32),
            dma((LOADS,)), dma((6,)), dma((2,)), dma((3,)),
            dma((8,)), dma((8,)), dma((7,)), dma((7,)),
            dma((8,)), dma((8,)), dma((7,)), dma((7,)),
            dma((8,)), dma((8,)), dma((7,)), dma((7,)),
            dma((8,)), dma((8,)), dma((7,)), dma((7,)),
            dma((GROUP,)), dma((GROUP,)), dma((GROUP,)),
            dma((GROUP,)), dma((GROUP,)), dma((GROUP,)),
        ],
        compiler_params=pltpu.CompilerParams(
            collective_id=0, has_side_effects=True, vmem_limit_bytes=50 * 1024 * 1024
        ),
    )(
        features.reshape(nodes // SIDE, SIDE, width), weight, adj_tiles,
        tile_row, tile_col, tile_count, cotangent,
    )
    return act, fgrad, wgrad.reshape(weight.shape)


def solution(mesh):
    in_specs = (
        P(("col", "row"), None),
        P(),
        P("row", "col", None, None, None),
        P("row", "col", None),
        P("row", "col", None),
        P("row", "col"),
        P(("row", "col"), None),
    )
    out_specs = (P(("row", "col"), None), P(("col", "row"), None), P())
    return jax.shard_map(body, mesh=mesh, in_specs=in_specs, out_specs=out_specs, check_vma=False)
```

```python
import math

import jax
import jax.numpy as jnp
from jax import lax
from jax.experimental import pallas as pl
from jax.experimental.pallas import tpu as pltpu
from jax.sharding import PartitionSpec as P

F32 = jnp.float32
BF16 = jnp.bfloat16
MESH = pl.DeviceIdType.MESH

SIDE = 128
BLOCKS = 32
SLOTS = 384
PAIRS = (SLOTS + BLOCKS) // 2
ENTRIES = 512
GROUP = 16
HALF = SIDE // 2
UNROLL = 26
TURNS = PAIRS // UNROLL
LOADS = 8
ZERO = BLOCKS
TILE, SOURCE, KEEP, LAST, SOME = range(5)


def upright(flat, lanes):
    column = jnp.transpose(jnp.broadcast_to(flat, (SIDE, flat.shape[1])))
    return jnp.concatenate([column] * (lanes // SIDE), axis=1)


def over_rows(condition, value):
    return jnp.sum(jnp.where(condition, value, 0), axis=0, keepdims=True)


def plan_pairs(place, pick, total):
    def counts(shape):
        return [lax.broadcasted_iota(jnp.int32, shape, d) for d in range(2)]

    place_up = upright(place, SLOTS)
    down, across = counts((SLOTS, SLOTS))
    rank = over_rows((place_up == place) & (down < total) & (down < across), 1)
    down, across = counts((SLOTS, SIDE))
    tiles = over_rows((place_up[:, :SIDE] == across) & (down < total), 1)
    pairs = (tiles + 1) // 2
    pairs_up = upright(pairs, SIDE)
    down, across = counts((SIDE, SIDE))
    first = over_rows(down < across, pairs_up)
    first_up = upright(first, ENTRIES)
    down, across = counts((BLOCKS, SLOTS))
    spot = rank + 2 * over_rows(down == place, first_up[:BLOCKS, :SLOTS])
    spot = jnp.where(lax.broadcasted_iota(jnp.int32, (1, SLOTS), 1) < total, spot, -1)
    down, across = counts((SLOTS, ENTRIES))
    found = upright(spot, ENTRIES) == across
    tile = over_rows(found, down)
    source = over_rows(found, upright(pick, ENTRIES) - ZERO) + ZERO
    down, across = counts((BLOCKS, ENTRIES))
    pairs_up = jnp.concatenate([pairs_up[:BLOCKS]] * (ENTRIES // SIDE), axis=1)
    keep = 1 - over_rows((first_up[:BLOCKS] == across) & (pairs_up > 0), 1)
    return tile, source, keep, jnp.maximum(first + pairs - 1, 0), jnp.minimum(pairs, 1)


def kernel(
    feat_hbm, weight_hbm, adj_hbm, row_hbm, col_hbm, count_hbm, cot_hbm,
    act_hbm, fgrad_hbm, wgrad_hbm,
    tiles, sums, xs, gs_a, gs_b, weight, cot, rows, cols, plan_v, act_v, fgrad_v,
    col_out, col_in, col_sum, col_land, row_out, row_in, row_sum, row_land,
    fgrad_t, wt, wt_land, wpart, wpart_land, wgrad_v,
    plan_f, plan_b, count,
    load_sem, small_sem, plan_sem, out_sem,
    ag1_send, ag1_recv, ag1f_send, ag1f_recv,
    rsx_send, rsx_recv, rsz_send, rsz_recv,
    ag2_send, ag2_recv, ag2f_send, ag2f_recv,
    rsc_send, rsc_recv, rsr_send, rsr_recv,
    w1_send, w1_recv, w2_send, w2_recv, w3_send, w3_recv,
):
    r = lax.axis_index("row")
    c = lax.axis_index("col")
    core, chip = r % 2, r // 2
    xlo, y = chip // 4, chip % 4
    xhi, z = c % 2, c // 2
    sibling = (2 * chip + (1 - core), c)
    partner = (r, 2 * z + (1 - xhi))

    def chip_at(k, sign):
        return 4 * ((xlo + k // 4) % 2) + (y + sign * (k % 4) + 4) % 4

    def z_at(k, sign):
        return (z + sign * k + 8) % 8

    def remote(src, dst, send, recv, device):
        return pltpu.make_async_remote_copy(
            src_ref=src, dst_ref=dst, send_sem=send, recv_sem=recv,
            device_id=device, device_id_type=MESH,
        )

    barrier = pltpu.get_barrier_semaphore()
    for k in range(1, GROUP):
        pl.semaphore_signal(barrier, inc=1, device_id=((r + k) % GROUP, c), device_id_type=MESH)
        pl.semaphore_signal(barrier, inc=1, device_id=(r, (c + k) % GROUP), device_id_type=MESH)

    smalls = [
        pltpu.make_async_copy(row_hbm.at[0, 0], rows.at[0], small_sem.at[0]),
        pltpu.make_async_copy(col_hbm.at[0, 0], cols.at[0], small_sem.at[1]),
        pltpu.make_async_copy(count_hbm, count, small_sem.at[2]),
        pltpu.make_async_copy(feat_hbm, xs.at[pl.ds(2 * r, 2)], small_sem.at[3]),
        pltpu.make_async_copy(weight_hbm, weight, small_sem.at[4]),
        pltpu.make_async_copy(cot_hbm, cot, small_sem.at[5]),
    ]
    for copy in smalls:
        copy.start()
    part = SLOTS // LOADS
    loads = [
        pltpu.make_async_copy(
            adj_hbm.at[0, 0, pl.ds(i * part, part)], tiles.at[pl.ds(i * part, part)], load_sem.at[i]
        )
        for i in range(LOADS)
    ]
    for copy in loads:
        copy.start()
    xs[ZERO] = jnp.zeros((SIDE, SIDE), BF16)
    gs = (gs_a, gs_b)
    for f in range(2):
        gs[f][ZERO] = jnp.zeros((HALF, SIDE), BF16)
    pl.semaphore_wait(barrier, 2 * (GROUP - 1))

    pending = []
    here = pl.ds(2 * r, 2)
    for k in range(8):
        device = sibling if k == 0 else (2 * chip_at(k, 1) + core, c)
        copy = remote(feat_hbm, xs.at[here], ag1_send.at[k], ag1_recv.at[k], device)
        copy.start()
        pending.append(copy)

    for copy in smalls[:3]:
        copy.wait()
    total = count[0, 0]
    plan_v[...] = jnp.zeros_like(plan_v)
    for i, (place, pick, ready) in enumerate(((rows, cols, plan_f), (cols, rows, plan_b))):
        listed = plan_pairs(place[...], pick[...], total)
        for j, value in enumerate(listed):
            plan_v[i, j : j + 1, : value.shape[1]] = value
        pltpu.make_async_copy(plan_v.at[i], ready, plan_sem.at[i]).start()

    forwards = []
    for k in range(1, 8):
        slot = xs.at[pl.ds(2 * (2 * chip_at(k, -1) + core), 2)]
        remote(slot, slot, ag1_send.at[k], ag1_recv.at[k], sibling).wait_recv()
        copy = remote(slot, slot, ag1f_send.at[k - 1], ag1f_recv.at[k - 1], sibling)
        copy.start()
        forwards.append(copy)
    slot = xs.at[pl.ds(2 * (2 * chip + 1 - core), 2)]
    remote(slot, slot, ag1_send.at[0], ag1_recv.at[0], sibling).wait_recv()
    for k in range(1, 8):
        slot = xs.at[pl.ds(2 * (2 * chip_at(k, -1) + 1 - core), 2)]
        remote(slot, slot, ag1f_send.at[k - 1], ag1f_recv.at[k - 1], sibling).wait_recv()
    for copy in smalls[3:]:
        copy.wait()
    for i in range(2):
        pltpu.make_async_copy(plan_v.at[i], (plan_f, plan_b)[i], plan_sem.at[i]).wait()
    for copy in loads:
        copy.wait()
    for copy in pending + forwards:
        copy.wait_send()

    def tile_pass(listed, source, forward, half=0, service=None):
        height = SIDE if forward else HALF
        here = pl.ds(half * HALF, height)

        def some_pairs(turn, total):
            for u in range(UNROLL):
                p = turn * UNROLL + u
                one, two = tiles[listed[TILE, 2 * p]], tiles[listed[TILE, 2 * p + 1]]
                with_one, with_two = source[listed[SOURCE, 2 * p]], source[listed[SOURCE, 2 * p + 1]]
                if forward:
                    left = jnp.concatenate([one, two], axis=1)
                    right = jnp.concatenate([with_one, with_two], axis=0)
                else:
                    left = jnp.concatenate([with_one, with_two], axis=1)
                    right = jnp.concatenate([one, two], axis=0)
                product = jnp.dot(left, right, preferred_element_type=F32)
                total = total * listed[KEEP, p].astype(F32) + product
                sums[p, here, :] = total
            if service is not None:
                service(turn)
            return total

        lax.fori_loop(0, TURNS, some_pairs, jnp.zeros((height, SIDE), F32))

    def block_sum(listed, b, rows=slice(None)):
        return sums[listed[LAST, b], rows, :] * listed[SOME, b].astype(F32)

    tile_pass(plan_f, xs, True)
    order = (4, 3, 5, 2, 6, 1, 7, 0)
    pending = []
    for k in order:
        for h in range(2):
            b = 2 * (2 * z_at(k, 1) + 1 - xhi) + h
            col_out[k, h] = block_sum(plan_f, b).astype(BF16)
        copy = remote(col_out.at[k], col_in.at[k], rsx_send.at[k], rsx_recv.at[k], partner)
        copy.start()
        pending.append(copy)
    own = []
    for k in order:
        mine = [block_sum(plan_f, 2 * (2 * z_at(k, 1) + xhi) + h) for h in range(2)]
        remote(col_in.at[k], col_in.at[k], rsx_send.at[k], rsx_recv.at[k], partner).wait_recv()
        mine = [mine[h] + col_in[k, h].astype(F32) for h in range(2)]
        if k == 0:
            own = mine
        else:
            for h in range(2):
                col_sum[k, h] = mine[h].astype(BF16)
            copy = remote(
                col_sum.at[k], col_land.at[k], rsz_send.at[k - 1], rsz_recv.at[k - 1],
                (r, 2 * z_at(k, 1) + xhi),
            )
            copy.start()
            pending.append(copy)
    for k in (1, 7, 2, 6, 3, 5, 4):
        remote(
            col_land.at[k], col_land.at[k], rsz_send.at[k - 1], rsz_recv.at[k - 1], partner
        ).wait_recv()
        own = [own[h] + col_land[k, h].astype(F32) for h in range(2)]

    aggregated = jnp.concatenate(own, axis=0).astype(BF16)
    w = weight[...]
    preact = jnp.dot(aggregated, w, preferred_element_type=F32)
    sigma = jax.nn.sigmoid(preact)
    slope = sigma * (1.0 + preact * (1.0 - sigma))
    pre_grad = (cot[...].astype(F32) * slope).astype(BF16)
    agg_grad = lax.dot_general(
        w, pre_grad, (((1,), (1,)), ((), ())), preferred_element_type=F32
    ).astype(BF16)
    for f in range(2):
        for h in range(2):
            gs[f][2 * c + h] = agg_grad[f * HALF : (f + 1) * HALF, h * SIDE : (h + 1) * SIDE]

    def nodes_of(at, other):
        across = 1 - xhi if other else xhi
        return pl.ds(2 * (2 * at + across), 2)

    def spread(f, k):
        slot = gs[f].at[nodes_of(z, False)]
        device = partner if k == 0 else (r, 2 * z_at(k, 1) + xhi)
        copy = remote(slot, slot, ag2_send.at[f, k], ag2_recv.at[f, k], device)
        copy.start()
        pending.append(copy)

    def hand_on(f, k):
        slot = gs[f].at[nodes_of(z_at(k, -1), False)]
        remote(slot, slot, ag2_send.at[f, k], ag2_recv.at[f, k], partner).wait_recv()
        remote(slot, slot, ag2f_send.at[f, k], ag2f_recv.at[f, k], partner).start()

    def gathered(f):
        slot = gs[f].at[nodes_of(z, True)]
        remote(slot, slot, ag2_send.at[f, 0], ag2_recv.at[f, 0], partner).wait_recv()
        for k in ahead:
            slot = gs[f].at[nodes_of(z_at(k, -1), True)]
            remote(slot, slot, ag2f_send.at[f, k], ag2f_recv.at[f, k], partner).wait_recv()
            slot = gs[f].at[nodes_of(z_at(k, -1), False)]
            pending.append(remote(slot, slot, ag2f_send.at[f, k], ag2f_recv.at[f, k], partner))

    ahead = (1, 7, 2, 6, 3, 5, 4)
    for k in ahead + (0,):
        spread(0, k)

    act_v[...] = (preact * sigma).astype(BF16)
    act_out = pltpu.make_async_copy(act_v, act_hbm, out_sem.at[0])
    act_out.start()
    terms = lax.dot_general(
        aggregated, pre_grad, (((0,), (0,)), ((), ())), preferred_element_type=F32
    )
    for q in range(GROUP):
        wt[q] = terms[8 * q : 8 * q + 8]
    for k in range(1, GROUP):
        to = (r + k) % GROUP
        copy = remote(wt.at[to], wt_land.at[k], w1_send.at[k], w1_recv.at[k], (to, c))
        copy.start()
        pending.append(copy)

    for k in ahead:
        hand_on(0, k)
        spread(1, k)
    spread(1, 0)
    gathered(0)

    def hand_on_one(turn):
        @pl.when(turn < 7)
        def _():
            step = turn // 2
            hand_on(1, (1 - turn % 2) * (step + 1) + (turn % 2) * (7 - step))

    def reduce_rows(f):
        rows = pl.ds(f * HALF, HALF)
        for k in order:
            for h in range(2):
                b = 2 * (2 * chip_at(k, 1) + 1 - core) + h
                row_out[f, k, h] = block_sum(plan_b, b, rows).astype(BF16)
            copy = remote(
                row_out.at[f, k], row_in.at[f, k], rsc_send.at[f, k], rsc_recv.at[f, k], sibling
            )
            copy.start()
            pending.append(copy)
        for k in order:
            mine = [block_sum(plan_b, 2 * (2 * chip_at(k, 1) + core) + h, rows) for h in range(2)]
            remote(
                row_in.at[f, k], row_in.at[f, k], rsc_send.at[f, k], rsc_recv.at[f, k], sibling
            ).wait_recv()
            mine = [mine[h] + row_in[f, k, h].astype(F32) for h in range(2)]
            if k == 0:
                for h in range(2):
                    fgrad_t[h, rows, :] = mine[h]
            else:
                for h in range(2):
                    row_sum[f, k, h] = mine[h].astype(BF16)
                copy = remote(
                    row_sum.at[f, k], row_land.at[f, k], rsr_send.at[f, k], rsr_recv.at[f, k],
                    (2 * chip_at(k, 1) + core, c),
                )
                copy.start()
                pending.append(copy)

    order = (2, 6, 1, 3, 5, 7, 4, 0)
    tile_pass(plan_b, gs[0], False, 0, hand_on_one)
    reduce_rows(0)
    term = wt[r]
    for k in range(1, GROUP):
        land = wt_land.at[k]
        remote(land, land, w1_send.at[k], w1_recv.at[k], partner).wait_recv()
        term = term + wt_land[k]
    wpart[...] = term
    for k in range(1, GROUP):
        copy = remote(
            wpart, wpart_land.at[k], w2_send.at[k], w2_recv.at[k], (r, (c + k) % GROUP)
        )
        copy.start()
        pending.append(copy)
    gathered(1)

    def finish_weight(turn):
        @pl.when(turn == TURNS // 2)
        def _():
            term = wpart[...]
            for k in range(1, GROUP):
                land = wpart_land.at[k]
                remote(land, land, w2_send.at[k], w2_recv.at[k], partner).wait_recv()
                term = term + wpart_land[k]
            wgrad_v[r] = term * (1.0 / math.sqrt(SIDE * BLOCKS * GROUP))
            for k in range(1, GROUP):
                slot = wgrad_v.at[r]
                remote(slot, slot, w3_send.at[k], w3_recv.at[k], ((r + k) % GROUP, c)).start()

    tile_pass(plan_b, gs[1], False, 1, finish_weight)
    reduce_rows(1)
    for k in range(1, GROUP):
        slot = wgrad_v.at[(r - k + GROUP) % GROUP]
        copy = remote(slot, slot, w3_send.at[k], w3_recv.at[k], ((r + k) % GROUP, c))
        copy.wait_recv()
        pending.append(copy)
    wgrad_out = pltpu.make_async_copy(wgrad_v, wgrad_hbm, out_sem.at[2])
    wgrad_out.start()

    own = [fgrad_t[h] for h in range(2)]
    for k in (1, 3, 4, 2, 5, 7, 6):
        for f in range(2):
            land = row_land.at[f, k]
            remote(land, land, rsr_send.at[f, k], rsr_recv.at[f, k], sibling).wait_recv()
        for h in range(2):
            parts = [row_land[f, k, h].astype(F32) for f in range(2)]
            own[h] = own[h] + jnp.concatenate(parts, axis=0)
    for h in range(2):
        fgrad_v[h * SIDE : (h + 1) * SIDE, :] = own[h].T.astype(BF16)
    fgrad_out = pltpu.make_async_copy(fgrad_v, fgrad_hbm, out_sem.at[1])
    fgrad_out.start()
    for copy in pending:
        copy.wait_send()
    act_out.wait()
    fgrad_out.wait()
    wgrad_out.wait()


def body(features, weight, adj_tiles, tile_row, tile_col, tile_count, cotangent):
    nodes, width = features.shape
    hidden = weight.shape[1]
    any_spec = pl.BlockSpec(memory_space=pl.ANY)
    dma = pltpu.SemaphoreType.DMA
    in_hbm = lambda array: pltpu.with_memory_space_constraint(array, pltpu.HBM)
    blocks = lambda *lead: pltpu.VMEM((*lead, SIDE, SIDE), BF16)
    halves = lambda *lead: pltpu.VMEM((*lead, HALF, SIDE), BF16)
    act, fgrad, wgrad = pl.pallas_call(
        kernel,
        out_shape=(
            jax.ShapeDtypeStruct((nodes, hidden), BF16),
            jax.ShapeDtypeStruct((nodes, width), BF16),
            jax.ShapeDtypeStruct((GROUP, 8, hidden), F32),
        ),
        in_specs=[any_spec] * 7,
        out_specs=(any_spec,) * 3,
        scratch_shapes=[
            blocks(SLOTS),
            pltpu.VMEM((PAIRS, SIDE, SIDE), F32),
            blocks(BLOCKS + 1),
            halves(BLOCKS + 1),
            halves(BLOCKS + 1),
            pltpu.VMEM((width, hidden), BF16),
            pltpu.VMEM((nodes, hidden), BF16),
            pltpu.VMEM((1, SLOTS), jnp.int32),
            pltpu.VMEM((1, SLOTS), jnp.int32),
            pltpu.VMEM((2, 8, ENTRIES), jnp.int32),
            pltpu.VMEM((nodes, hidden), BF16),
            pltpu.VMEM((nodes, width), BF16),
            blocks(8, 2), blocks(8, 2), blocks(8, 2), blocks(8, 2),
            halves(2, 8, 2), halves(2, 8, 2), halves(2, 8, 2), halves(2, 8, 2),
            pltpu.VMEM((2, SIDE, SIDE), F32),
            pltpu.VMEM((GROUP, 8, hidden), F32),
            pltpu.VMEM((GROUP, 8, hidden), F32),
            pltpu.VMEM((8, hidden), F32),
            pltpu.VMEM((GROUP, 8, hidden), F32),
            pltpu.VMEM((GROUP, 8, hidden), F32),
            pltpu.SMEM((8, ENTRIES), jnp.int32),
            pltpu.SMEM((8, ENTRIES), jnp.int32),
            pltpu.SMEM((1, 1), jnp.int32),
            dma((LOADS,)), dma((6,)), dma((2,)), dma((3,)),
            dma((8,)), dma((8,)), dma((7,)), dma((7,)),
            dma((8,)), dma((8,)), dma((7,)), dma((7,)),
            dma((2, 8)), dma((2, 8)), dma((2, 8)), dma((2, 8)),
            dma((2, 8)), dma((2, 8)), dma((2, 8)), dma((2, 8)),
            dma((GROUP,)), dma((GROUP,)), dma((GROUP,)),
            dma((GROUP,)), dma((GROUP,)), dma((GROUP,)),
        ],
        compiler_params=pltpu.CompilerParams(
            collective_id=0, has_side_effects=True, vmem_limit_bytes=50 * 1024 * 1024
        ),
    )(
        in_hbm(features.reshape(nodes // SIDE, SIDE, width)), in_hbm(weight), in_hbm(adj_tiles),
        in_hbm(tile_row), in_hbm(tile_col), tile_count, in_hbm(cotangent),
    )
    return act, fgrad, wgrad.reshape(weight.shape)


def solution(mesh):
    in_specs = (
        P(("col", "row"), None),
        P(),
        P("row", "col", None, None, None),
        P("row", "col", None),
        P("row", "col", None),
        P("row", "col"),
        P(("row", "col"), None),
    )
    out_specs = (P(("row", "col"), None), P(("col", "row"), None), P())
    return jax.shard_map(body, mesh=mesh, in_specs=in_specs, out_specs=out_specs, check_vma=False)
```

```python
import math

import jax
import jax.numpy as jnp
from jax import lax
from jax.experimental import pallas as pl
from jax.experimental.pallas import tpu as pltpu
from jax.sharding import PartitionSpec as P

F32 = jnp.float32
BF16 = jnp.bfloat16
MESH = pl.DeviceIdType.MESH

SIDE = 128
BLOCKS = 32
SLOTS = 384
PAIRS = (SLOTS + BLOCKS) // 2
ENTRIES = 512
GROUP = 16
HALF = SIDE // 2
UNROLL = 26
TURNS = PAIRS // UNROLL
EARLY = (5, 7)
LOADS = 8
ZERO = BLOCKS
TILE, SOURCE, KEEP, LAST, SOME = range(5)


def upright(flat, lanes):
    column = jnp.transpose(jnp.broadcast_to(flat, (SIDE, flat.shape[1])))
    return jnp.concatenate([column] * (lanes // SIDE), axis=1)


def over_rows(condition, value):
    return jnp.sum(jnp.where(condition, value, 0), axis=0, keepdims=True)


def plan_pairs(place, pick, total):
    def counts(shape):
        return [lax.broadcasted_iota(jnp.int32, shape, d) for d in range(2)]

    place_up = upright(place, SLOTS)
    down, across = counts((SLOTS, SLOTS))
    rank = over_rows((place_up == place) & (down < total) & (down < across), 1)
    down, across = counts((SLOTS, SIDE))
    tiles = over_rows((place_up[:, :SIDE] == across) & (down < total), 1)
    pairs = (tiles + 1) // 2
    pairs_up = upright(pairs, SIDE)
    down, across = counts((SIDE, SIDE))
    first = over_rows(down < across, pairs_up)
    first_up = upright(first, ENTRIES)
    down, across = counts((BLOCKS, SLOTS))
    spot = rank + 2 * over_rows(down == place, first_up[:BLOCKS, :SLOTS])
    spot = jnp.where(lax.broadcasted_iota(jnp.int32, (1, SLOTS), 1) < total, spot, -1)
    down, across = counts((SLOTS, ENTRIES))
    found = upright(spot, ENTRIES) == across
    tile = over_rows(found, down)
    source = over_rows(found, upright(pick, ENTRIES) - ZERO) + ZERO
    down, across = counts((BLOCKS, ENTRIES))
    pairs_up = jnp.concatenate([pairs_up[:BLOCKS]] * (ENTRIES // SIDE), axis=1)
    keep = 1 - over_rows((first_up[:BLOCKS] == across) & (pairs_up > 0), 1)
    return tile, source, keep, jnp.maximum(first + pairs - 1, 0), jnp.minimum(pairs, 1)


def kernel(
    feat_hbm, weight_hbm, adj_hbm, row_hbm, col_hbm, count_hbm, cot_hbm,
    act_hbm, fgrad_hbm, wgrad_hbm,
    tiles, sums, xs, gs_a, gs_b, weight, cot, rows, cols, plan_v, act_v, fgrad_v,
    col_out, col_in, col_sum, col_land, row_out, row_in, row_sum, row_land,
    agg_own, fgrad_t, wt, wt_land, wpart, wpart_land, wgrad_v,
    plan_f, plan_b, count,
    load_sem, small_sem, plan_sem, out_sem,
    ag1_send, ag1_recv, ag1f_send, ag1f_recv,
    rsx_send, rsx_recv, rsz_send, rsz_recv,
    ag2_send, ag2_recv, ag2f_send, ag2f_recv,
    rsc_send, rsc_recv, rsr_send, rsr_recv,
    w_send, w_recv,
):
    r = lax.axis_index("row")
    c = lax.axis_index("col")
    core, chip = r % 2, r // 2
    xlo, y = chip // 4, chip % 4
    xhi, z = c % 2, c // 2
    sibling = (2 * chip + (1 - core), c)
    partner = (r, 2 * z + (1 - xhi))
    gs = (gs_a, gs_b)

    def chip_at(k, sign):
        return 4 * ((xlo + k // 4) % 2) + (y + sign * (k % 4) + 4) % 4

    def z_at(k, sign):
        return (z + sign * k + 8) % 8

    def remote(src, dst, send, recv, device):
        return pltpu.make_async_remote_copy(
            src_ref=src, dst_ref=dst, send_sem=send, recv_sem=recv,
            device_id=device, device_id_type=MESH,
        )

    def all_sent(whole, sem):
        remote(whole, whole, sem, sem, partner).wait_send()

    def all_here(whole, sem):
        remote(whole, whole, sem, sem, partner).wait_recv()

    barrier = pltpu.get_barrier_semaphore()
    for k in range(1, GROUP):
        pl.semaphore_signal(barrier, inc=1, device_id=((r + k) % GROUP, c), device_id_type=MESH)
        pl.semaphore_signal(barrier, inc=1, device_id=(r, (c + k) % GROUP), device_id_type=MESH)

    smalls = [
        pltpu.make_async_copy(row_hbm.at[0, 0], rows.at[0], small_sem.at[0]),
        pltpu.make_async_copy(col_hbm.at[0, 0], cols.at[0], small_sem.at[1]),
        pltpu.make_async_copy(count_hbm, count, small_sem.at[2]),
        pltpu.make_async_copy(feat_hbm, xs.at[pl.ds(2 * r, 2)], small_sem.at[3]),
        pltpu.make_async_copy(weight_hbm, weight, small_sem.at[4]),
        pltpu.make_async_copy(cot_hbm, cot, small_sem.at[5]),
    ]
    for copy in smalls:
        copy.start()
    part = SLOTS // LOADS
    loads = [
        pltpu.make_async_copy(
            adj_hbm.at[0, 0, pl.ds(i * part, part)], tiles.at[pl.ds(i * part, part)], load_sem.at[i]
        )
        for i in range(LOADS)
    ]
    for copy in loads:
        copy.start()
    xs[ZERO] = jnp.zeros((SIDE, SIDE), BF16)
    for f in range(2):
        gs[f][ZERO] = jnp.zeros((HALF, SIDE), BF16)
    pl.semaphore_wait(barrier, 2 * (GROUP - 1))

    here = pl.ds(2 * r, 2)
    for k in (1, 4, 3, 5, 7, 2, 6, 0):
        device = sibling if k == 0 else (2 * chip_at(k, 1) + core, c)
        remote(feat_hbm, xs.at[here], ag1_send, ag1_recv.at[k], device).start()

    for copy in smalls[:3]:
        copy.wait()
    total = count[0, 0]
    plan_v[...] = jnp.zeros_like(plan_v)
    for i, (place, pick, ready) in enumerate(((rows, cols, plan_f), (cols, rows, plan_b))):
        listed = plan_pairs(place[...], pick[...], total)
        for j, value in enumerate(listed):
            plan_v[i, j : j + 1, : value.shape[1]] = value
        pltpu.make_async_copy(plan_v.at[i], ready, plan_sem.at[i]).start()

    for k in (1, 4, 3, 5, 7, 2, 6):
        slot = xs.at[pl.ds(2 * (2 * chip_at(k, -1) + core), 2)]
        remote(slot, slot, ag1_send, ag1_recv.at[k], sibling).wait_recv()
        remote(slot, slot, ag1f_send, ag1f_recv, sibling).start()
    slot = xs.at[pl.ds(2 * (2 * chip + 1 - core), 2)]
    remote(slot, slot, ag1_send, ag1_recv.at[0], sibling).wait_recv()
    for copy in smalls[3:]:
        copy.wait()
    for i in range(2):
        pltpu.make_async_copy(plan_v.at[i], (plan_f, plan_b)[i], plan_sem.at[i]).wait()
    for copy in loads:
        copy.wait()
    all_sent(xs.at[pl.ds(0, 16)], ag1_send)
    all_here(xs.at[pl.ds(0, 14)], ag1f_recv)

    def rows_of(half):
        return pl.ds(half * HALF, HALF)

    def tile_pass(listed, source, forward, half, service):
        here = rows_of(half)

        def some_pairs(turn, total):
            for u in range(UNROLL):
                p = turn * UNROLL + u
                with_one, with_two = source[listed[SOURCE, 2 * p]], source[listed[SOURCE, 2 * p + 1]]
                if forward:
                    one, two = tiles[listed[TILE, 2 * p], here], tiles[listed[TILE, 2 * p + 1], here]
                    left = jnp.concatenate([one, two], axis=1)
                    right = jnp.concatenate([with_one, with_two], axis=0)
                else:
                    one, two = tiles[listed[TILE, 2 * p]], tiles[listed[TILE, 2 * p + 1]]
                    left = jnp.concatenate([with_one, with_two], axis=1)
                    right = jnp.concatenate([one, two], axis=0)
                product = jnp.dot(left, right, preferred_element_type=F32)
                total = total * listed[KEEP, p].astype(F32) + product
                sums[p, here, :] = total
            if service is not None:
                service(turn)
            return total

        lax.fori_loop(0, TURNS, some_pairs, jnp.zeros((HALF, SIDE), F32))

    def block_sum(listed, b, here):
        return sums[listed[LAST, b], here, :] * listed[SOME, b].astype(F32)

    order = (4, 3, 5, 2, 6, 1, 7, 0)

    def send_columns(f):
        for k in order:
            for h in range(2):
                b = 2 * (2 * z_at(k, 1) + 1 - xhi) + h
                col_out[f, k, h] = block_sum(plan_f, b, rows_of(f)).astype(BF16)
            remote(
                col_out.at[f, k], col_in.at[f, k], rsx_send.at[f], rsx_recv.at[f, k], partner
            ).start()

    def pass_columns(f, k):
        blocks = [2 * (2 * z_at(k, 1) + xhi) + h for h in range(2)]
        mine = [block_sum(plan_f, b, rows_of(f)) for b in blocks]
        come = col_in.at[f, k]
        remote(come, come, rsx_send.at[f], rsx_recv.at[f, k], partner).wait_recv()
        for h in range(2):
            both = mine[h] + col_in[f, k, h].astype(F32)
            if k == 0:
                agg_own[h, rows_of(f), :] = both
            else:
                col_sum[f, k - 1, h] = both.astype(BF16)
        if k != 0:
            remote(
                col_sum.at[f, k - 1], col_land.at[f, k - 1], rsz_send.at[f], rsz_recv.at[f],
                (r, 2 * z_at(k, 1) + xhi),
            ).start()

    def begin_columns(turn):
        for i, at in enumerate(EARLY):
            @pl.when(turn == at)
            def _():
                pass_columns(0, order[i])

    tile_pass(plan_f, xs, True, 0, None)
    send_columns(0)
    tile_pass(plan_f, xs, True, 1, begin_columns)
    send_columns(1)
    for k in order[len(EARLY) :]:
        pass_columns(0, k)
    for k in order:
        pass_columns(1, k)
    all_sent(xs.at[pl.ds(0, 14)], ag1f_send)
    for f in range(2):
        all_sent(col_out.at[f], rsx_send.at[f])
    for f in range(2):
        all_here(col_land.at[f], rsz_recv.at[f])
    own = [agg_own[h] for h in range(2)]
    for k in range(7):
        for h in range(2):
            parts = [col_land[f, k, h].astype(F32) for f in range(2)]
            own[h] = own[h] + jnp.concatenate(parts, axis=0)

    aggregated = jnp.concatenate(own, axis=0).astype(BF16)
    w = weight[...]
    preact = jnp.dot(aggregated, w, preferred_element_type=F32)
    sigma = jax.nn.sigmoid(preact)
    slope = sigma * (1.0 + preact * (1.0 - sigma))
    pre_grad = (cot[...].astype(F32) * slope).astype(BF16)
    agg_grad = lax.dot_general(
        w, pre_grad, (((1,), (1,)), ((), ())), preferred_element_type=F32
    ).astype(BF16)
    for f in range(2):
        for h in range(2):
            gs[f][2 * c + h] = agg_grad[f * HALF : (f + 1) * HALF, h * SIDE : (h + 1) * SIDE]

    def nodes_of(at, other):
        across = 1 - xhi if other else xhi
        return pl.ds(2 * (2 * at + across), 2)

    def spread(f, k):
        slot = gs[f].at[nodes_of(z, False)]
        if k == 0:
            remote(slot, slot, ag2_send.at[f], ag2f_recv.at[f], partner).start()
        else:
            device = (r, 2 * z_at(k, 1) + xhi)
            remote(slot, slot, ag2_send.at[f], ag2_recv.at[f, k], device).start()

    def hand_on(f, k):
        slot = gs[f].at[nodes_of(z_at(k, -1), False)]
        remote(slot, slot, ag2_send.at[f], ag2_recv.at[f, k], partner).wait_recv()
        remote(slot, slot, ag2f_send.at[f], ag2f_recv.at[f], partner).start()

    ahead = (1, 7, 2, 6, 3, 5, 4)
    for k in ahead + (0,):
        spread(0, k)

    act_v[...] = (preact * sigma).astype(BF16)
    act_out = pltpu.make_async_copy(act_v, act_hbm, out_sem.at[0])
    act_out.start()
    terms = lax.dot_general(
        aggregated, pre_grad, (((0,), (0,)), ((), ())), preferred_element_type=F32
    )
    for q in range(GROUP):
        wt[q] = terms[8 * q : 8 * q + 8]
    for k in range(1, GROUP):
        to = (r + k) % GROUP
        remote(wt.at[to], wt_land.at[k - 1], w_send.at[0], w_recv.at[0], (to, c)).start()

    for k in ahead:
        hand_on(0, k)
        spread(1, k)
    spread(1, 0)
    for f in range(2):
        all_sent(col_sum.at[f], rsz_send.at[f])
    all_here(gs[0].at[pl.ds(0, 16)], ag2f_recv.at[0])

    def hand_on_one(turn):
        @pl.when(turn < 7)
        def _():
            step = turn // 2
            hand_on(1, (1 - turn % 2) * (step + 1) + (turn % 2) * (7 - step))

    def reduce_rows(f):
        for k in turns:
            for h in range(2):
                b = 2 * (2 * chip_at(k, 1) + 1 - core) + h
                row_out[f, k, h] = block_sum(plan_b, b, rows_of(f)).astype(BF16)
            remote(
                row_out.at[f, k], row_in.at[f, k], rsc_send.at[f], rsc_recv.at[f, k], sibling
            ).start()
        for k in turns:
            blocks = [2 * (2 * chip_at(k, 1) + core) + h for h in range(2)]
            mine = [block_sum(plan_b, b, rows_of(f)) for b in blocks]
            come = row_in.at[f, k]
            remote(come, come, rsc_send.at[f], rsc_recv.at[f, k], sibling).wait_recv()
            for h in range(2):
                both = mine[h] + row_in[f, k, h].astype(F32)
                if k == 0:
                    fgrad_t[h, rows_of(f), :] = both
                else:
                    row_sum[f, k - 1, h] = both.astype(BF16)
            if k != 0:
                remote(
                    row_sum.at[f, k - 1], row_land.at[f, k - 1], rsr_send.at[f], rsr_recv.at[f],
                    (2 * chip_at(k, 1) + core, c),
                ).start()

    turns = (2, 6, 1, 3, 5, 7, 4, 0)
    tile_pass(plan_b, gs[0], False, 0, hand_on_one)
    reduce_rows(0)
    all_here(wt_land, w_recv.at[0])
    term = wt[r]
    for k in range(GROUP - 1):
        term = term + wt_land[k]
    wpart[...] = term
    for k in range(1, GROUP):
        device = (r, (c + k) % GROUP)
        remote(wpart, wpart_land.at[k - 1], w_send.at[1], w_recv.at[1], device).start()
    all_here(gs[1].at[pl.ds(0, 16)], ag2f_recv.at[1])

    def finish_weight(turn):
        @pl.when(turn == TURNS // 2)
        def _():
            all_here(wpart_land, w_recv.at[1])
            term = wpart[...]
            for k in range(GROUP - 1):
                term = term + wpart_land[k]
            wgrad_v[r] = term * (1.0 / math.sqrt(SIDE * BLOCKS * GROUP))
            slot = wgrad_v.at[r]
            for k in range(1, GROUP):
                remote(slot, slot, w_send.at[2], w_recv.at[2], ((r + k) % GROUP, c)).start()

    tile_pass(plan_b, gs[1], False, 1, finish_weight)
    reduce_rows(1)
    others = pl.ds(0, GROUP - 1)
    all_here(wgrad_v.at[others], w_recv.at[2])
    wgrad_out = pltpu.make_async_copy(wgrad_v, wgrad_hbm, out_sem.at[2])
    wgrad_out.start()
    for i in range(3):
        all_sent(wt.at[others], w_send.at[i])
    for f in range(2):
        all_sent(gs[f].at[pl.ds(0, 16)], ag2_send.at[f])
        all_sent(gs[f].at[pl.ds(0, 14)], ag2f_send.at[f])
        all_sent(row_out.at[f], rsc_send.at[f])
    act_out.wait()

    own = [fgrad_t[h] for h in range(2)]
    for f in range(2):
        all_here(row_land.at[f], rsr_recv.at[f])
    for k in range(7):
        for h in range(2):
            parts = [row_land[f, k, h].astype(F32) for f in range(2)]
            own[h] = own[h] + jnp.concatenate(parts, axis=0)
    for h in range(2):
        fgrad_v[h * SIDE : (h + 1) * SIDE, :] = own[h].T.astype(BF16)
    fgrad_out = pltpu.make_async_copy(fgrad_v, fgrad_hbm, out_sem.at[1])
    fgrad_out.start()
    for f in range(2):
        all_sent(row_sum.at[f], rsr_send.at[f])
    wgrad_out.wait()
    fgrad_out.wait()


def body(features, weight, adj_tiles, tile_row, tile_col, tile_count, cotangent):
    nodes, width = features.shape
    hidden = weight.shape[1]
    any_spec = pl.BlockSpec(memory_space=pl.ANY)
    dma = pltpu.SemaphoreType.DMA
    in_hbm = lambda array: pltpu.with_memory_space_constraint(array, pltpu.HBM)
    blocks = lambda *lead: pltpu.VMEM((*lead, SIDE, SIDE), BF16)
    halves = lambda *lead: pltpu.VMEM((*lead, HALF, SIDE), BF16)
    act, fgrad, wgrad = pl.pallas_call(
        kernel,
        out_shape=(
            jax.ShapeDtypeStruct((nodes, hidden), BF16),
            jax.ShapeDtypeStruct((nodes, width), BF16),
            jax.ShapeDtypeStruct((GROUP, 8, hidden), F32),
        ),
        in_specs=[any_spec] * 7,
        out_specs=(any_spec,) * 3,
        scratch_shapes=[
            blocks(SLOTS),
            pltpu.VMEM((PAIRS, SIDE, SIDE), F32),
            blocks(BLOCKS + 1),
            halves(BLOCKS + 1),
            halves(BLOCKS + 1),
            pltpu.VMEM((width, hidden), BF16),
            pltpu.VMEM((nodes, hidden), BF16),
            pltpu.VMEM((1, SLOTS), jnp.int32),
            pltpu.VMEM((1, SLOTS), jnp.int32),
            pltpu.VMEM((2, 8, ENTRIES), jnp.int32),
            pltpu.VMEM((nodes, hidden), BF16),
            pltpu.VMEM((nodes, width), BF16),
            halves(2, 8, 2), halves(2, 8, 2), halves(2, 7, 2), halves(2, 7, 2),
            halves(2, 8, 2), halves(2, 8, 2), halves(2, 7, 2), halves(2, 7, 2),
            pltpu.VMEM((2, SIDE, SIDE), F32),
            pltpu.VMEM((2, SIDE, SIDE), F32),
            pltpu.VMEM((GROUP, 8, hidden), F32),
            pltpu.VMEM((GROUP - 1, 8, hidden), F32),
            pltpu.VMEM((8, hidden), F32),
            pltpu.VMEM((GROUP - 1, 8, hidden), F32),
            pltpu.VMEM((GROUP, 8, hidden), F32),
            pltpu.SMEM((8, ENTRIES), jnp.int32),
            pltpu.SMEM((8, ENTRIES), jnp.int32),
            pltpu.SMEM((1, 1), jnp.int32),
            dma((LOADS,)), dma((6,)), dma((2,)), dma((3,)),
            dma, dma((8,)), dma, dma,
            dma((2,)), dma((2, 8)), dma((2,)), dma((2,)),
            dma((2,)), dma((2, 8)), dma((2,)), dma((2,)),
            dma((2,)), dma((2, 8)), dma((2,)), dma((2,)),
            dma((3,)), dma((3,)),
        ],
        compiler_params=pltpu.CompilerParams(
            collective_id=0, has_side_effects=True, vmem_limit_bytes=50 * 1024 * 1024
        ),
    )(
        in_hbm(features.reshape(nodes // SIDE, SIDE, width)), in_hbm(weight), in_hbm(adj_tiles),
        in_hbm(tile_row), in_hbm(tile_col), tile_count, in_hbm(cotangent),
    )
    return act, fgrad, wgrad.reshape(weight.shape)


def solution(mesh):
    in_specs = (
        P(("col", "row"), None),
        P(),
        P("row", "col", None, None, None),
        P("row", "col", None),
        P("row", "col", None),
        P("row", "col"),
        P(("row", "col"), None),
    )
    out_specs = (P(("row", "col"), None), P(("col", "row"), None), P())
    return jax.shard_map(body, mesh=mesh, in_specs=in_specs, out_specs=out_specs, check_vma=False)
```

```python
import math

import jax
import jax.numpy as jnp
from jax import lax
from jax.experimental import pallas as pl
from jax.experimental.pallas import tpu as pltpu
from jax.sharding import PartitionSpec as P

F32 = jnp.float32
BF16 = jnp.bfloat16
MESH = pl.DeviceIdType.MESH

SIDE = 128
BLOCKS = 32
SLOTS = 384
PAIRS = (SLOTS + BLOCKS) // 2
ENTRIES = 512
GROUP = 16
HALF = SIDE // 2
UNROLL = 26
LONG = 104
TURNS = PAIRS // UNROLL
EARLY = (5, 7)
LOADS = 8
ZERO = BLOCKS
TILE, SOURCE, KEEP, LAST, SOME = range(5)


def upright(flat, lanes):
    column = jnp.transpose(jnp.broadcast_to(flat, (SIDE, flat.shape[1])))
    return jnp.concatenate([column] * (lanes // SIDE), axis=1)


def over_rows(condition, value):
    return jnp.sum(jnp.where(condition, value, 0), axis=0, keepdims=True)


def plan_pairs(place, pick, total):
    def counts(shape):
        return [lax.broadcasted_iota(jnp.int32, shape, d) for d in range(2)]

    place_up = upright(place, SLOTS)
    down, across = counts((SLOTS, SLOTS))
    rank = over_rows((place_up == place) & (down < total) & (down < across), 1)
    down, across = counts((SLOTS, SIDE))
    tiles = over_rows((place_up[:, :SIDE] == across) & (down < total), 1)
    pairs = (tiles + 1) // 2
    pairs_up = upright(pairs, SIDE)
    down, across = counts((SIDE, SIDE))
    first = over_rows(down < across, pairs_up)
    first_up = upright(first, ENTRIES)
    down, across = counts((BLOCKS, SLOTS))
    spot = rank + 2 * over_rows(down == place, first_up[:BLOCKS, :SLOTS])
    spot = jnp.where(lax.broadcasted_iota(jnp.int32, (1, SLOTS), 1) < total, spot, -1)
    down, across = counts((SLOTS, ENTRIES))
    found = upright(spot, ENTRIES) == across
    tile = over_rows(found, down)
    source = over_rows(found, upright(pick, ENTRIES) - ZERO) + ZERO
    down, across = counts((BLOCKS, ENTRIES))
    pairs_up = jnp.concatenate([pairs_up[:BLOCKS]] * (ENTRIES // SIDE), axis=1)
    keep = 1 - over_rows((first_up[:BLOCKS] == across) & (pairs_up > 0), 1)
    return tile, source, keep, jnp.maximum(first + pairs - 1, 0), jnp.minimum(pairs, 1)


def kernel(
    feat_hbm, weight_hbm, adj_hbm, row_hbm, col_hbm, count_hbm, cot_hbm,
    act_hbm, fgrad_hbm, wgrad_hbm,
    tiles, sums, xs, gs_a, gs_b, weight, cot, rows, cols, plan_v, act_v, fgrad_v,
    col_out, col_in, col_sum, col_land, row_out, row_in, row_sum, row_land,
    agg_own, fgrad_t, wt, wt_land, wpart, wnear, wpart_land, wgrad_v,
    plan_f, plan_b, count,
    load_sem, small_sem, plan_sem, out_sem,
    ag1_send, ag1_recv, ag1f_send, ag1f_recv,
    rsx_send, rsx_recv, rsz_send, rsz_recv,
    ag2_send, ag2_recv, ag2f_send, ag2f_recv,
    rsc_send, rsc_recv, rsr_send, rsr_recv,
    w_send, w_recv,
):
    r = lax.axis_index("row")
    c = lax.axis_index("col")
    core, chip = r % 2, r // 2
    xlo, y = chip // 4, chip % 4
    xhi, z = c % 2, c // 2
    sibling = (2 * chip + (1 - core), c)
    partner = (r, 2 * z + (1 - xhi))
    gs = (gs_a, gs_b)

    def chip_at(k, sign):
        return 4 * ((xlo + k // 4) % 2) + (y + sign * (k % 4) + 4) % 4

    def z_at(k, sign):
        return (z + sign * k + 8) % 8

    def remote(src, dst, send, recv, device):
        return pltpu.make_async_remote_copy(
            src_ref=src, dst_ref=dst, send_sem=send, recv_sem=recv,
            device_id=device, device_id_type=MESH,
        )

    def all_sent(whole, sem):
        remote(whole, whole, sem, sem, partner).wait_send()

    def all_here(whole, sem):
        remote(whole, whole, sem, sem, partner).wait_recv()

    barrier = pltpu.get_barrier_semaphore()
    for k in range(1, GROUP):
        pl.semaphore_signal(barrier, inc=1, device_id=((r + k) % GROUP, c), device_id_type=MESH)
        pl.semaphore_signal(barrier, inc=1, device_id=(r, (c + k) % GROUP), device_id_type=MESH)

    smalls = [
        pltpu.make_async_copy(row_hbm.at[0, 0], rows.at[0], small_sem.at[0]),
        pltpu.make_async_copy(col_hbm.at[0, 0], cols.at[0], small_sem.at[1]),
        pltpu.make_async_copy(count_hbm, count, small_sem.at[2]),
        pltpu.make_async_copy(feat_hbm, xs.at[pl.ds(2 * r, 2)], small_sem.at[3]),
        pltpu.make_async_copy(weight_hbm, weight, small_sem.at[4]),
        pltpu.make_async_copy(cot_hbm, cot, small_sem.at[5]),
    ]
    for copy in smalls:
        copy.start()
    part = SLOTS // LOADS
    loads = [
        pltpu.make_async_copy(
            adj_hbm.at[0, 0, pl.ds(i * part, part)], tiles.at[pl.ds(i * part, part)], load_sem.at[i]
        )
        for i in range(LOADS)
    ]
    for copy in loads:
        copy.start()
    xs[ZERO] = jnp.zeros((SIDE, SIDE), BF16)
    for f in range(2):
        gs[f][ZERO] = jnp.zeros((HALF, SIDE), BF16)
    pl.semaphore_wait(barrier, 2 * (GROUP - 1))

    here = pl.ds(2 * r, 2)
    for k in (1, 4, 3, 5, 7, 2, 6, 0):
        device = sibling if k == 0 else (2 * chip_at(k, 1) + core, c)
        remote(feat_hbm, xs.at[here], ag1_send, ag1_recv.at[k], device).start()

    for copy in smalls[:3]:
        copy.wait()
    total = count[0, 0]
    plan_v[...] = jnp.zeros_like(plan_v)
    for i, (place, pick, ready) in enumerate(((rows, cols, plan_f), (cols, rows, plan_b))):
        listed = plan_pairs(place[...], pick[...], total)
        for j, value in enumerate(listed):
            plan_v[i, j : j + 1, : value.shape[1]] = value
        pltpu.make_async_copy(plan_v.at[i], ready, plan_sem.at[i]).start()

    for k in (1, 4, 3, 5, 7, 2, 6):
        slot = xs.at[pl.ds(2 * (2 * chip_at(k, -1) + core), 2)]
        remote(slot, slot, ag1_send, ag1_recv.at[k], sibling).wait_recv()
        remote(slot, slot, ag1f_send, ag1f_recv, sibling).start()
    slot = xs.at[pl.ds(2 * (2 * chip + 1 - core), 2)]
    remote(slot, slot, ag1_send, ag1_recv.at[0], sibling).wait_recv()
    for copy in smalls[3:]:
        copy.wait()
    for i in range(2):
        pltpu.make_async_copy(plan_v.at[i], (plan_f, plan_b)[i], plan_sem.at[i]).wait()
    for copy in loads:
        copy.wait()
    all_sent(xs.at[pl.ds(0, 16)], ag1_send)
    all_here(xs.at[pl.ds(0, 14)], ag1f_recv)

    def rows_of(half):
        return pl.ds(half * HALF, HALF)

    def tile_pass(listed, source, forward, half, service):
        unroll = LONG if service is None else UNROLL
        here = rows_of(half)

        def some_pairs(turn, total):
            for u in range(unroll):
                p = turn * unroll + u
                with_one, with_two = source[listed[SOURCE, 2 * p]], source[listed[SOURCE, 2 * p + 1]]
                if forward:
                    one, two = tiles[listed[TILE, 2 * p], here], tiles[listed[TILE, 2 * p + 1], here]
                    left = jnp.concatenate([one, two], axis=1)
                    right = jnp.concatenate([with_one, with_two], axis=0)
                else:
                    one, two = tiles[listed[TILE, 2 * p]], tiles[listed[TILE, 2 * p + 1]]
                    left = jnp.concatenate([with_one, with_two], axis=1)
                    right = jnp.concatenate([one, two], axis=0)
                product = jnp.dot(left, right, preferred_element_type=F32)
                total = total * listed[KEEP, p].astype(F32) + product
                sums[p, here, :] = total
            if service is not None:
                service(turn)
            return total

        lax.fori_loop(0, PAIRS // unroll, some_pairs, jnp.zeros((HALF, SIDE), F32))

    def block_sum(listed, b, here):
        return sums[listed[LAST, b], here, :] * listed[SOME, b].astype(F32)

    order = (4, 3, 5, 2, 6, 1, 7, 0)

    def send_columns(f):
        for k in order:
            for h in range(2):
                b = 2 * (2 * z_at(k, 1) + 1 - xhi) + h
                col_out[f, k, h] = block_sum(plan_f, b, rows_of(f)).astype(BF16)
            remote(
                col_out.at[f, k], col_in.at[f, k], rsx_send.at[f], rsx_recv.at[f, k], partner
            ).start()

    def pass_columns(f, k):
        blocks = [2 * (2 * z_at(k, 1) + xhi) + h for h in range(2)]
        mine = [block_sum(plan_f, b, rows_of(f)) for b in blocks]
        come = col_in.at[f, k]
        remote(come, come, rsx_send.at[f], rsx_recv.at[f, k], partner).wait_recv()
        for h in range(2):
            both = mine[h] + col_in[f, k, h].astype(F32)
            if k == 0:
                agg_own[h, rows_of(f), :] = both
            else:
                col_sum[f, k - 1, h] = both.astype(BF16)
        if k != 0:
            remote(
                col_sum.at[f, k - 1], col_land.at[f, k - 1], rsz_send.at[f], rsz_recv.at[f],
                (r, 2 * z_at(k, 1) + xhi),
            ).start()

    def begin_columns(turn):
        for i, at in enumerate(EARLY):
            @pl.when(turn == at)
            def _():
                pass_columns(0, order[i])

    tile_pass(plan_f, xs, True, 0, None)
    send_columns(0)
    tile_pass(plan_f, xs, True, 1, begin_columns)
    send_columns(1)
    for k in order[len(EARLY) :]:
        pass_columns(0, k)
    for k in order:
        pass_columns(1, k)
    all_sent(xs.at[pl.ds(0, 14)], ag1f_send)
    for f in range(2):
        all_sent(col_out.at[f], rsx_send.at[f])
    for f in range(2):
        all_here(col_land.at[f], rsz_recv.at[f])
    own = [agg_own[h] for h in range(2)]
    for k in range(7):
        for h in range(2):
            parts = [col_land[f, k, h].astype(F32) for f in range(2)]
            own[h] = own[h] + jnp.concatenate(parts, axis=0)

    aggregated = jnp.concatenate(own, axis=0).astype(BF16)
    w = weight[...]
    preact = jnp.dot(aggregated, w, preferred_element_type=F32)
    sigma = jax.nn.sigmoid(preact)
    slope = sigma * (1.0 + preact * (1.0 - sigma))
    pre_grad = (cot[...].astype(F32) * slope).astype(BF16)
    agg_grad = lax.dot_general(
        w, pre_grad, (((1,), (1,)), ((), ())), preferred_element_type=F32
    ).astype(BF16)
    for f in range(2):
        for h in range(2):
            gs[f][2 * c + h] = agg_grad[f * HALF : (f + 1) * HALF, h * SIDE : (h + 1) * SIDE]

    def nodes_of(at, other):
        across = 1 - xhi if other else xhi
        return pl.ds(2 * (2 * at + across), 2)

    def spread(f, k):
        slot = gs[f].at[nodes_of(z, False)]
        if k == 0:
            remote(slot, slot, ag2_send.at[f], ag2f_recv.at[f], partner).start()
        else:
            device = (r, 2 * z_at(k, 1) + xhi)
            remote(slot, slot, ag2_send.at[f], ag2_recv.at[f, k], device).start()

    def hand_on(f, k):
        slot = gs[f].at[nodes_of(z_at(k, -1), False)]
        remote(slot, slot, ag2_send.at[f], ag2_recv.at[f, k], partner).wait_recv()
        remote(slot, slot, ag2f_send.at[f], ag2f_recv.at[f], partner).start()

    ahead = (1, 7, 2, 6, 3, 5, 4)
    for k in (0,) + ahead:
        spread(0, k)
    spread(1, 0)

    act_v[...] = (preact * sigma).astype(BF16)
    act_out = pltpu.make_async_copy(act_v, act_hbm, out_sem.at[0])
    act_out.start()
    for k in ahead:
        hand_on(0, k)
        spread(1, k)
    terms = lax.dot_general(
        aggregated, pre_grad, (((0,), (0,)), ((), ())), preferred_element_type=F32
    )
    for q in range(GROUP):
        wt[q] = terms[8 * q : 8 * q + 8]
    for k in range(1, GROUP):
        to = (r + k) % GROUP
        remote(wt.at[to], wt_land.at[k - 1], w_send.at[0], w_recv.at[0], (to, c)).start()
    for f in range(2):
        all_sent(col_sum.at[f], rsz_send.at[f])
    all_here(gs[0].at[pl.ds(0, 16)], ag2f_recv.at[0])

    def hand_on_one(turn):
        @pl.when(turn < 7)
        def _():
            step = turn // 2
            hand_on(1, (1 - turn % 2) * (step + 1) + (turn % 2) * (7 - step))

    def reduce_rows(f):
        for k in turns:
            for h in range(2):
                b = 2 * (2 * chip_at(k, 1) + 1 - core) + h
                row_out[f, k, h] = block_sum(plan_b, b, rows_of(f)).astype(BF16)
            remote(
                row_out.at[f, k], row_in.at[f, k], rsc_send.at[f], rsc_recv.at[f, k], sibling
            ).start()
        for k in turns:
            blocks = [2 * (2 * chip_at(k, 1) + core) + h for h in range(2)]
            mine = [block_sum(plan_b, b, rows_of(f)) for b in blocks]
            come = row_in.at[f, k]
            remote(come, come, rsc_send.at[f], rsc_recv.at[f, k], sibling).wait_recv()
            for h in range(2):
                both = mine[h] + row_in[f, k, h].astype(F32)
                if k == 0:
                    fgrad_t[h, rows_of(f), :] = both
                else:
                    row_sum[f, k - 1, h] = both.astype(BF16)
            if k != 0:
                remote(
                    row_sum.at[f, k - 1], row_land.at[f, k - 1], rsr_send.at[f], rsr_recv.at[f],
                    (2 * chip_at(k, 1) + core, c),
                ).start()

    turns = (2, 6, 1, 3, 5, 7, 4, 0)
    tile_pass(plan_b, gs[0], False, 0, hand_on_one)
    reduce_rows(0)
    all_here(wt_land, w_recv.at[0])
    term = wt[r]
    for k in range(GROUP - 1):
        term = term + wt_land[k]
    wpart[...] = term
    wnear[...] = jnp.concatenate([term[:, :SIDE], term[:, SIDE:]], axis=0).astype(BF16)
    for k in range(1, GROUP):
        device = (r, (c + k) % GROUP)
        remote(wnear, wpart_land.at[k - 1], w_send.at[1], w_recv.at[1], device).start()
    all_here(gs[1].at[pl.ds(0, 16)], ag2f_recv.at[1])

    tile_pass(plan_b, gs[1], False, 1, None)
    reduce_rows(1)

    all_here(wpart_land, w_recv.at[1])
    far = wpart_land[0].astype(F32)
    for k in range(1, GROUP - 1):
        far = far + wpart_land[k].astype(F32)
    term = wpart[...] + jnp.concatenate([far[:8], far[8:]], axis=1)
    wgrad_v[r] = term * (1.0 / math.sqrt(SIDE * BLOCKS * GROUP))
    for k in range(1, GROUP):
        slot = wgrad_v.at[r]
        remote(slot, slot, w_send.at[2], w_recv.at[2], ((r + k) % GROUP, c)).start()
    others = pl.ds(0, GROUP - 1)
    all_here(wgrad_v.at[others], w_recv.at[2])
    wgrad_out = pltpu.make_async_copy(wgrad_v, wgrad_hbm, out_sem.at[2])
    wgrad_out.start()
    for i in range(3):
        all_sent(wpart_land if i == 1 else wt.at[others], w_send.at[i])
    for f in range(2):
        all_sent(gs[f].at[pl.ds(0, 16)], ag2_send.at[f])
        all_sent(gs[f].at[pl.ds(0, 14)], ag2f_send.at[f])
        all_sent(row_out.at[f], rsc_send.at[f])
    act_out.wait()

    own = [fgrad_t[h] for h in range(2)]
    for f in range(2):
        all_here(row_land.at[f], rsr_recv.at[f])
    for k in range(7):
        for h in range(2):
            parts = [row_land[f, k, h].astype(F32) for f in range(2)]
            own[h] = own[h] + jnp.concatenate(parts, axis=0)
    for h in range(2):
        fgrad_v[h * SIDE : (h + 1) * SIDE, :] = own[h].T.astype(BF16)
    fgrad_out = pltpu.make_async_copy(fgrad_v, fgrad_hbm, out_sem.at[1])
    fgrad_out.start()
    for f in range(2):
        all_sent(row_sum.at[f], rsr_send.at[f])
    wgrad_out.wait()
    fgrad_out.wait()


def body(features, weight, adj_tiles, tile_row, tile_col, tile_count, cotangent):
    nodes, width = features.shape
    hidden = weight.shape[1]
    any_spec = pl.BlockSpec(memory_space=pl.ANY)
    dma = pltpu.SemaphoreType.DMA
    in_hbm = lambda array: pltpu.with_memory_space_constraint(array, pltpu.HBM)
    blocks = lambda *lead: pltpu.VMEM((*lead, SIDE, SIDE), BF16)
    halves = lambda *lead: pltpu.VMEM((*lead, HALF, SIDE), BF16)
    act, fgrad, wgrad = pl.pallas_call(
        kernel,
        out_shape=(
            jax.ShapeDtypeStruct((nodes, hidden), BF16),
            jax.ShapeDtypeStruct((nodes, width), BF16),
            jax.ShapeDtypeStruct((GROUP, 8, hidden), F32),
        ),
        in_specs=[any_spec] * 7,
        out_specs=(any_spec,) * 3,
        scratch_shapes=[
            blocks(SLOTS),
            pltpu.VMEM((PAIRS, SIDE, SIDE), F32),
            blocks(BLOCKS + 1),
            halves(BLOCKS + 1),
            halves(BLOCKS + 1),
            pltpu.VMEM((width, hidden), BF16),
            pltpu.VMEM((nodes, hidden), BF16),
            pltpu.VMEM((1, SLOTS), jnp.int32),
            pltpu.VMEM((1, SLOTS), jnp.int32),
            pltpu.VMEM((2, 8, ENTRIES), jnp.int32),
            pltpu.VMEM((nodes, hidden), BF16),
            pltpu.VMEM((nodes, width), BF16),
            halves(2, 8, 2), halves(2, 8, 2), halves(2, 7, 2), halves(2, 7, 2),
            halves(2, 8, 2), halves(2, 8, 2), halves(2, 7, 2), halves(2, 7, 2),
            pltpu.VMEM((2, SIDE, SIDE), F32),
            pltpu.VMEM((2, SIDE, SIDE), F32),
            pltpu.VMEM((GROUP, 8, hidden), F32),
            pltpu.VMEM((GROUP - 1, 8, hidden), F32),
            pltpu.VMEM((8, hidden), F32),
            pltpu.VMEM((16, SIDE), BF16),
            pltpu.VMEM((GROUP - 1, 16, SIDE), BF16),
            pltpu.VMEM((GROUP, 8, hidden), F32),
            pltpu.SMEM((8, ENTRIES), jnp.int32),
            pltpu.SMEM((8, ENTRIES), jnp.int32),
            pltpu.SMEM((1, 1), jnp.int32),
            dma((LOADS,)), dma((6,)), dma((2,)), dma((3,)),
            dma, dma((8,)), dma, dma,
            dma((2,)), dma((2, 8)), dma((2,)), dma((2,)),
            dma((2,)), dma((2, 8)), dma((2,)), dma((2,)),
            dma((2,)), dma((2, 8)), dma((2,)), dma((2,)),
            dma((3,)), dma((3,)),
        ],
        compiler_params=pltpu.CompilerParams(
            collective_id=0, has_side_effects=True, vmem_limit_bytes=50 * 1024 * 1024
        ),
    )(
        in_hbm(features.reshape(nodes // SIDE, SIDE, width)), in_hbm(weight), in_hbm(adj_tiles),
        in_hbm(tile_row), in_hbm(tile_col), tile_count, in_hbm(cotangent),
    )
    return act, fgrad, wgrad.reshape(weight.shape)


def solution(mesh):
    in_specs = (
        P(("col", "row"), None),
        P(),
        P("row", "col", None, None, None),
        P("row", "col", None),
        P("row", "col", None),
        P("row", "col"),
        P(("row", "col"), None),
    )
    out_specs = (P(("row", "col"), None), P(("col", "row"), None), P())
    return jax.shard_map(body, mesh=mesh, in_specs=in_specs, out_specs=out_specs, check_vma=False)
```

```python
import math

import jax
import jax.numpy as jnp
from jax import lax
from jax.experimental import pallas as pl
from jax.experimental.pallas import tpu as pltpu
from jax.sharding import PartitionSpec as P

F32 = jnp.float32
BF16 = jnp.bfloat16
MESH = pl.DeviceIdType.MESH

SIDE = 128
BLOCKS = 32
SLOTS = 384
PAIRS = (SLOTS + BLOCKS) // 2
ENTRIES = 512
GROUP = 16
HALF = SIDE // 2
UNROLL = 26
LONG = 104
TURNS = PAIRS // UNROLL
EARLY = (2, 3)
LOADS = 8
ZERO = BLOCKS
TILE, SOURCE, KEEP, LAST, SOME = range(5)


def upright(flat, lanes):
    column = jnp.transpose(jnp.broadcast_to(flat, (SIDE, flat.shape[1])))
    return jnp.concatenate([column] * (lanes // SIDE), axis=1)


def over_rows(condition, value):
    return jnp.sum(jnp.where(condition, value, 0), axis=0, keepdims=True)


def plan_pairs(place, pick, total):
    def counts(shape):
        return [lax.broadcasted_iota(jnp.int32, shape, d) for d in range(2)]

    place_up = upright(place, SLOTS)
    down, across = counts((SLOTS, SLOTS))
    rank = over_rows((place_up == place) & (down < total) & (down < across), 1)
    down, across = counts((SLOTS, SIDE))
    tiles = over_rows((place_up[:, :SIDE] == across) & (down < total), 1)
    pairs = (tiles + 1) // 2
    pairs_up = upright(pairs, SIDE)
    down, across = counts((SIDE, SIDE))
    first = over_rows(down < across, pairs_up)
    first_up = upright(first, ENTRIES)
    down, across = counts((BLOCKS, SLOTS))
    spot = rank + 2 * over_rows(down == place, first_up[:BLOCKS, :SLOTS])
    spot = jnp.where(lax.broadcasted_iota(jnp.int32, (1, SLOTS), 1) < total, spot, -1)
    down, across = counts((SLOTS, ENTRIES))
    found = upright(spot, ENTRIES) == across
    tile = over_rows(found, down)
    source = over_rows(found, upright(pick, ENTRIES) - ZERO) + ZERO
    down, across = counts((BLOCKS, ENTRIES))
    pairs_up = jnp.concatenate([pairs_up[:BLOCKS]] * (ENTRIES // SIDE), axis=1)
    keep = 1 - over_rows((first_up[:BLOCKS] == across) & (pairs_up > 0), 1)
    return tile, source, keep, jnp.maximum(first + pairs - 1, 0), jnp.minimum(pairs, 1)


def kernel(
    feat_hbm, weight_hbm, adj_hbm, row_hbm, col_hbm, count_hbm, cot_hbm,
    act_hbm, fgrad_hbm, wgrad_hbm,
    tiles, sums, xs, gs_a, gs_b, weight, cot, rows, cols, plan_v, act_v, fgrad_v,
    col_out, col_in, col_sum, col_land, row_out, row_in, row_sum, row_land,
    agg_own, fgrad_t, wt, wt_land, wpart, wnear, wpart_land, wgrad_v,
    plan_f, plan_b, count,
    load_sem, small_sem, plan_sem, out_sem,
    ag1_send, ag1_recv, ag1f_send, ag1f_recv,
    rsx_send, rsx_recv, rsz_send, rsz_recv,
    ag2_send, ag2_recv, ag2f_send, ag2f_recv,
    rsc_send, rsc_recv, rsr_send, rsr_recv,
    w_send, w_recv,
):
    r = lax.axis_index("row")
    c = lax.axis_index("col")
    core, chip = r % 2, r // 2
    xlo, y = chip // 4, chip % 4
    xhi, z = c % 2, c // 2
    sibling = (2 * chip + (1 - core), c)
    partner = (r, 2 * z + (1 - xhi))
    gs = (gs_a, gs_b)

    def chip_at(k, sign):
        return 4 * ((xlo + k // 4) % 2) + (y + sign * (k % 4) + 4) % 4

    def z_at(k, sign):
        return (z + sign * k + 8) % 8

    def remote(src, dst, send, recv, device):
        return pltpu.make_async_remote_copy(
            src_ref=src, dst_ref=dst, send_sem=send, recv_sem=recv,
            device_id=device, device_id_type=MESH,
        )

    def all_sent(whole, sem):
        remote(whole, whole, sem, sem, partner).wait_send()

    def all_here(whole, sem):
        remote(whole, whole, sem, sem, partner).wait_recv()

    barrier = pltpu.get_barrier_semaphore()
    for k in range(1, GROUP):
        pl.semaphore_signal(barrier, inc=1, device_id=((r + k) % GROUP, c), device_id_type=MESH)
        pl.semaphore_signal(barrier, inc=1, device_id=(r, (c + k) % GROUP), device_id_type=MESH)

    smalls = [
        pltpu.make_async_copy(row_hbm.at[0, 0], rows.at[0], small_sem.at[0]),
        pltpu.make_async_copy(col_hbm.at[0, 0], cols.at[0], small_sem.at[1]),
        pltpu.make_async_copy(count_hbm, count, small_sem.at[2]),
        pltpu.make_async_copy(feat_hbm, xs.at[pl.ds(2 * r, 2)], small_sem.at[3]),
        pltpu.make_async_copy(weight_hbm, weight, small_sem.at[4]),
        pltpu.make_async_copy(cot_hbm, cot, small_sem.at[5]),
    ]
    for copy in smalls:
        copy.start()
    part = SLOTS // LOADS
    loads = [
        pltpu.make_async_copy(
            adj_hbm.at[0, 0, pl.ds(i * part, part)], tiles.at[pl.ds(i * part, part)], load_sem.at[i]
        )
        for i in range(LOADS)
    ]
    for copy in loads:
        copy.start()
    xs[ZERO] = jnp.zeros((SIDE, SIDE), BF16)
    for f in range(2):
        gs[f][ZERO] = jnp.zeros((HALF, SIDE), BF16)
    pl.semaphore_wait(barrier, 2 * (GROUP - 1))

    here = pl.ds(2 * r, 2)
    for k in (1, 4, 3, 5, 7, 2, 6, 0):
        device = sibling if k == 0 else (2 * chip_at(k, 1) + core, c)
        remote(feat_hbm, xs.at[here], ag1_send, ag1_recv.at[k], device).start()

    for copy in smalls[:3]:
        copy.wait()
    total = count[0, 0]
    plan_v[...] = jnp.zeros_like(plan_v)
    for i, (place, pick, ready) in enumerate(((rows, cols, plan_f), (cols, rows, plan_b))):
        listed = plan_pairs(place[...], pick[...], total)
        for j, value in enumerate(listed):
            plan_v[i, j : j + 1, : value.shape[1]] = value
        pltpu.make_async_copy(plan_v.at[i], ready, plan_sem.at[i]).start()

    for k in (1, 4, 3, 5, 7, 2, 6):
        slot = xs.at[pl.ds(2 * (2 * chip_at(k, -1) + core), 2)]
        remote(slot, slot, ag1_send, ag1_recv.at[k], sibling).wait_recv()
        remote(slot, slot, ag1f_send, ag1f_recv, sibling).start()
    slot = xs.at[pl.ds(2 * (2 * chip + 1 - core), 2)]
    remote(slot, slot, ag1_send, ag1_recv.at[0], sibling).wait_recv()
    for copy in smalls[3:]:
        copy.wait()
    for i in range(2):
        pltpu.make_async_copy(plan_v.at[i], (plan_f, plan_b)[i], plan_sem.at[i]).wait()
    for copy in loads:
        copy.wait()
    all_sent(xs.at[pl.ds(0, 16)], ag1_send)
    all_here(xs.at[pl.ds(0, 14)], ag1f_recv)

    def rows_of(half):
        return pl.ds(half * HALF, HALF)

    def tile_pass(listed, source, forward, half, service, unroll=LONG):
        here = rows_of(half)

        def some_pairs(turn, total):
            for u in range(unroll):
                p = turn * unroll + u
                with_one, with_two = source[listed[SOURCE, 2 * p]], source[listed[SOURCE, 2 * p + 1]]
                if forward:
                    one, two = tiles[listed[TILE, 2 * p], here], tiles[listed[TILE, 2 * p + 1], here]
                    left = jnp.concatenate([one, two], axis=1)
                    right = jnp.concatenate([with_one, with_two], axis=0)
                else:
                    one, two = tiles[listed[TILE, 2 * p]], tiles[listed[TILE, 2 * p + 1]]
                    left = jnp.concatenate([with_one, with_two], axis=1)
                    right = jnp.concatenate([one, two], axis=0)
                product = jnp.dot(left, right, preferred_element_type=F32)
                total = total * listed[KEEP, p].astype(F32) + product
                sums[p, here, :] = total
            if service is not None:
                service(turn)
            return total

        lax.fori_loop(0, PAIRS // unroll, some_pairs, jnp.zeros((HALF, SIDE), F32))

    def block_sum(listed, b, here):
        return sums[listed[LAST, b], here, :] * listed[SOME, b].astype(F32)

    order = (4, 3, 5, 2, 6, 1, 7, 0)

    def send_columns(f):
        for k in order:
            for h in range(2):
                b = 2 * (2 * z_at(k, 1) + 1 - xhi) + h
                col_out[f, k, h] = block_sum(plan_f, b, rows_of(f)).astype(BF16)
            remote(
                col_out.at[f, k], col_in.at[f, k], rsx_send.at[f], rsx_recv.at[f, k], partner
            ).start()

    def pass_columns(f, k):
        blocks = [2 * (2 * z_at(k, 1) + xhi) + h for h in range(2)]
        mine = [block_sum(plan_f, b, rows_of(f)) for b in blocks]
        come = col_in.at[f, k]
        remote(come, come, rsx_send.at[f], rsx_recv.at[f, k], partner).wait_recv()
        for h in range(2):
            both = mine[h] + col_in[f, k, h].astype(F32)
            if k == 0:
                agg_own[h, rows_of(f), :] = both
            else:
                col_sum[f, k - 1, h] = both.astype(BF16)
        if k != 0:
            remote(
                col_sum.at[f, k - 1], col_land.at[f, k - 1], rsz_send.at[f], rsz_recv.at[f],
                (r, 2 * z_at(k, 1) + xhi),
            ).start()

    def begin_columns(turn):
        for i, at in enumerate(EARLY):
            @pl.when(turn == at)
            def _():
                pass_columns(0, order[i])

    tile_pass(plan_f, xs, True, 0, None)
    send_columns(0)
    tile_pass(plan_f, xs, True, 1, begin_columns, 2 * UNROLL)
    send_columns(1)
    for k in order[len(EARLY) :]:
        pass_columns(0, k)
    for k in order:
        pass_columns(1, k)
    all_sent(xs.at[pl.ds(0, 14)], ag1f_send)
    for f in range(2):
        all_sent(col_out.at[f], rsx_send.at[f])
    for f in range(2):
        all_here(col_land.at[f], rsz_recv.at[f])
    own = [agg_own[h] for h in range(2)]
    for k in range(7):
        for h in range(2):
            parts = [col_land[f, k, h].astype(F32) for f in range(2)]
            own[h] = own[h] + jnp.concatenate(parts, axis=0)

    aggregated = jnp.concatenate(own, axis=0).astype(BF16)
    w = weight[...]
    preact = jnp.dot(aggregated, w, preferred_element_type=F32)
    sigma = jax.nn.sigmoid(preact)
    slope = sigma * (1.0 + preact * (1.0 - sigma))
    pre_grad = (cot[...].astype(F32) * slope).astype(BF16)
    agg_grad = lax.dot_general(
        w, pre_grad, (((1,), (1,)), ((), ())), preferred_element_type=F32
    ).astype(BF16)
    for f in range(2):
        for h in range(2):
            gs[f][2 * c + h] = agg_grad[f * HALF : (f + 1) * HALF, h * SIDE : (h + 1) * SIDE]

    def nodes_of(at, other):
        across = 1 - xhi if other else xhi
        return pl.ds(2 * (2 * at + across), 2)

    def spread(f, k):
        slot = gs[f].at[nodes_of(z, False)]
        if k == 0:
            remote(slot, slot, ag2_send.at[f], ag2f_recv.at[f], partner).start()
        else:
            device = (r, 2 * z_at(k, 1) + xhi)
            remote(slot, slot, ag2_send.at[f], ag2_recv.at[f, k], device).start()

    def hand_on(f, k):
        slot = gs[f].at[nodes_of(z_at(k, -1), False)]
        remote(slot, slot, ag2_send.at[f], ag2_recv.at[f, k], partner).wait_recv()
        remote(slot, slot, ag2f_send.at[f], ag2f_recv.at[f], partner).start()

    ahead = (1, 7, 2, 6, 3, 5, 4)
    for k in (0,) + ahead:
        spread(0, k)
    spread(1, 0)

    act_v[...] = (preact * sigma).astype(BF16)
    act_out = pltpu.make_async_copy(act_v, act_hbm, out_sem.at[0])
    act_out.start()
    for k in ahead:
        hand_on(0, k)
        spread(1, k)
    terms = lax.dot_general(
        aggregated, pre_grad, (((0,), (0,)), ((), ())), preferred_element_type=F32
    )
    for q in range(GROUP):
        wt[q] = terms[8 * q : 8 * q + 8]
    for k in range(1, GROUP):
        to = (r + k) % GROUP
        remote(wt.at[to], wt_land.at[k - 1], w_send.at[0], w_recv.at[0], (to, c)).start()
    for f in range(2):
        all_sent(col_sum.at[f], rsz_send.at[f])
    all_here(gs[0].at[pl.ds(0, 16)], ag2f_recv.at[0])

    def hand_on_one(turn):
        @pl.when(turn < 7)
        def _():
            step = turn // 2
            hand_on(1, (1 - turn % 2) * (step + 1) + (turn % 2) * (7 - step))

    def reduce_rows(f):
        for k in turns:
            for h in range(2):
                b = 2 * (2 * chip_at(k, 1) + 1 - core) + h
                row_out[f, k, h] = block_sum(plan_b, b, rows_of(f)).astype(BF16)
            remote(
                row_out.at[f, k], row_in.at[f, k], rsc_send.at[f], rsc_recv.at[f, k], sibling
            ).start()
        for k in turns:
            blocks = [2 * (2 * chip_at(k, 1) + core) + h for h in range(2)]
            mine = [block_sum(plan_b, b, rows_of(f)) for b in blocks]
            come = row_in.at[f, k]
            remote(come, come, rsc_send.at[f], rsc_recv.at[f, k], sibling).wait_recv()
            for h in range(2):
                both = mine[h] + row_in[f, k, h].astype(F32)
                if k == 0:
                    fgrad_t[h, rows_of(f), :] = both
                else:
                    row_sum[f, k - 1, h] = both.astype(BF16)
            if k != 0:
                remote(
                    row_sum.at[f, k - 1], row_land.at[f, k - 1], rsr_send.at[f], rsr_recv.at[f],
                    (2 * chip_at(k, 1) + core, c),
                ).start()

    turns = (2, 6, 1, 3, 5, 7, 4, 0)
    tile_pass(plan_b, gs[0], False, 0, hand_on_one, UNROLL)
    reduce_rows(0)
    all_here(wt_land, w_recv.at[0])
    term = wt[r]
    for k in range(GROUP - 1):
        term = term + wt_land[k]
    wpart[...] = term
    wnear[...] = jnp.concatenate([term[:, :SIDE], term[:, SIDE:]], axis=0).astype(BF16)
    for k in range(1, GROUP):
        device = (r, (c + k) % GROUP)
        remote(wnear, wpart_land.at[k - 1], w_send.at[1], w_recv.at[1], device).start()
    all_here(gs[1].at[pl.ds(0, 16)], ag2f_recv.at[1])

    tile_pass(plan_b, gs[1], False, 1, None)
    reduce_rows(1)

    all_here(wpart_land, w_recv.at[1])
    far = wpart_land[0].astype(F32)
    for k in range(1, GROUP - 1):
        far = far + wpart_land[k].astype(F32)
    term = wpart[...] + jnp.concatenate([far[:8], far[8:]], axis=1)
    wgrad_v[r] = term * (1.0 / math.sqrt(SIDE * BLOCKS * GROUP))
    for k in range(1, GROUP):
        slot = wgrad_v.at[r]
        remote(slot, slot, w_send.at[2], w_recv.at[2], ((r + k) % GROUP, c)).start()
    others = pl.ds(0, GROUP - 1)
    all_here(wgrad_v.at[others], w_recv.at[2])
    wgrad_out = pltpu.make_async_copy(wgrad_v, wgrad_hbm, out_sem.at[2])
    wgrad_out.start()
    for i in range(3):
        all_sent(wpart_land if i == 1 else wt.at[others], w_send.at[i])
    for f in range(2):
        all_sent(gs[f].at[pl.ds(0, 16)], ag2_send.at[f])
        all_sent(gs[f].at[pl.ds(0, 14)], ag2f_send.at[f])
        all_sent(row_out.at[f], rsc_send.at[f])
    act_out.wait()

    own = [fgrad_t[h] for h in range(2)]
    for f in range(2):
        all_here(row_land.at[f], rsr_recv.at[f])
    for k in range(7):
        for h in range(2):
            parts = [row_land[f, k, h].astype(F32) for f in range(2)]
            own[h] = own[h] + jnp.concatenate(parts, axis=0)
    for h in range(2):
        fgrad_v[h * SIDE : (h + 1) * SIDE, :] = own[h].T.astype(BF16)
    fgrad_out = pltpu.make_async_copy(fgrad_v, fgrad_hbm, out_sem.at[1])
    fgrad_out.start()
    for f in range(2):
        all_sent(row_sum.at[f], rsr_send.at[f])
    wgrad_out.wait()
    fgrad_out.wait()


def body(features, weight, adj_tiles, tile_row, tile_col, tile_count, cotangent):
    nodes, width = features.shape
    hidden = weight.shape[1]
    any_spec = pl.BlockSpec(memory_space=pl.ANY)
    dma = pltpu.SemaphoreType.DMA
    in_hbm = lambda array: pltpu.with_memory_space_constraint(array, pltpu.HBM)
    blocks = lambda *lead: pltpu.VMEM((*lead, SIDE, SIDE), BF16)
    halves = lambda *lead: pltpu.VMEM((*lead, HALF, SIDE), BF16)
    act, fgrad, wgrad = pl.pallas_call(
        kernel,
        out_shape=(
            jax.ShapeDtypeStruct((nodes, hidden), BF16),
            jax.ShapeDtypeStruct((nodes, width), BF16),
            jax.ShapeDtypeStruct((GROUP, 8, hidden), F32),
        ),
        in_specs=[any_spec] * 7,
        out_specs=(any_spec,) * 3,
        scratch_shapes=[
            blocks(SLOTS),
            pltpu.VMEM((PAIRS, SIDE, SIDE), F32),
            blocks(BLOCKS + 1),
            halves(BLOCKS + 1),
            halves(BLOCKS + 1),
            pltpu.VMEM((width, hidden), BF16),
            pltpu.VMEM((nodes, hidden), BF16),
            pltpu.VMEM((1, SLOTS), jnp.int32),
            pltpu.VMEM((1, SLOTS), jnp.int32),
            pltpu.VMEM((2, 8, ENTRIES), jnp.int32),
            pltpu.VMEM((nodes, hidden), BF16),
            pltpu.VMEM((nodes, width), BF16),
            halves(2, 8, 2), halves(2, 8, 2), halves(2, 7, 2), halves(2, 7, 2),
            halves(2, 8, 2), halves(2, 8, 2), halves(2, 7, 2), halves(2, 7, 2),
            pltpu.VMEM((2, SIDE, SIDE), F32),
            pltpu.VMEM((2, SIDE, SIDE), F32),
            pltpu.VMEM((GROUP, 8, hidden), F32),
            pltpu.VMEM((GROUP - 1, 8, hidden), F32),
            pltpu.VMEM((8, hidden), F32),
            pltpu.VMEM((16, SIDE), BF16),
            pltpu.VMEM((GROUP - 1, 16, SIDE), BF16),
            pltpu.VMEM((GROUP, 8, hidden), F32),
            pltpu.SMEM((8, ENTRIES), jnp.int32),
            pltpu.SMEM((8, ENTRIES), jnp.int32),
            pltpu.SMEM((1, 1), jnp.int32),
            dma((LOADS,)), dma((6,)), dma((2,)), dma((3,)),
            dma, dma((8,)), dma, dma,
            dma((2,)), dma((2, 8)), dma((2,)), dma((2,)),
            dma((2,)), dma((2, 8)), dma((2,)), dma((2,)),
            dma((2,)), dma((2, 8)), dma((2,)), dma((2,)),
            dma((3,)), dma((3,)),
        ],
        compiler_params=pltpu.CompilerParams(
            collective_id=0, has_side_effects=True, vmem_limit_bytes=50 * 1024 * 1024
        ),
    )(
        in_hbm(features.reshape(nodes // SIDE, SIDE, width)), in_hbm(weight), in_hbm(adj_tiles),
        in_hbm(tile_row), in_hbm(tile_col), tile_count, in_hbm(cotangent),
    )
    return act, fgrad, wgrad.reshape(weight.shape)


def solution(mesh):
    in_specs = (
        P(("col", "row"), None),
        P(),
        P("row", "col", None, None, None),
        P("row", "col", None),
        P("row", "col", None),
        P("row", "col"),
        P(("row", "col"), None),
    )
    out_specs = (P(("row", "col"), None), P(("col", "row"), None), P())
    return jax.shard_map(body, mesh=mesh, in_specs=in_specs, out_specs=out_specs, check_vma=False)
```
